128 devices in a mesh: emb: 8 (over y, core), seq: 16 (over x, z).
Axes of the slice: x: 4, y: 4, z: 4, core: 2. Of those that a mesh axis runs over, the one named last changes fastest.
Arguments:
- item_ids: int32 [128, 512], P(None, 'seq'), may hold values from 0 to 16383
- action_ids: int32 [128, 512], P(None, 'seq'), may hold values from 0 to 127
- hist_len: int32 [512], replicated, may hold values from 1 to 509, as said below
- hist_owner: int32 [512], replicated, may hold values from 0 to 127, as said below
- item_table: bfloat16 [16384, 1024], P(None, 'emb'), may hold values from -150 to 150
- action_table: bfloat16 [128, 1024], P(None, 'emb'), may hold values from -6 to 6
- w_in: bfloat16 [1024, 4096], replicated, may hold values from -0.1875 to 0.1875
- w_out: bfloat16 [1024, 1024], replicated, may hold values from -0.1875 to 0.1875
- cotangent: bfloat16 [65536, 1024], P(('emb', 'seq')), may hold values from -6 to 6
Outputs:
- history_out: bfloat16 [65536, 1024], P(('emb', 'seq'))
- row_grads: bfloat16 [128, 512, 1024], P(None, 'seq', 'emb')
- w_in_grad: float32 [1024, 4096], P(('emb', 'seq'))
- w_out_grad: float32 [1024, 1024], P(('emb', 'seq'))
The draws below stay inside these ranges and needn't reach their ends.
Inputs may be any that keep to these rules, and one draw needn't show every extreme that they name: `hist_len`: every owner has exactly 4 histories, whose lengths sum to at most 512; in every draw some owner's lengths sum to exactly 512. Ids at slots past an owner's histories are ignored. `hist_owner`: each owner number appears exactly 4 times.
All inputs are finite; a program needn't handle non-finite values.
Results may differ from the reference program's by a relative error of at most 0.015.
Values may be sent and summed in bfloat16 or wider, within the bound.
No kernel may reach another device: no remote copies, remote signals or barrier semaphores. Data moves between devices by JAX's collectives and lax.ppermute only.
A program may use at most 128 MiB of HBM per device.

```python
import math
import jax
import jax.numpy as jnp
import numpy as np
from jax import lax

D = 1024
HEADS = 4
HEAD = 256
ITEMS = 16384
ACTIONS = 128
CAP = 512
HPO = 4
OWNERS = 128


def history_plan(key):
    base = jax.random.fold_in(key, 11)
    pair_count = OWNERS // 2
    spare = jax.random.randint(jax.random.fold_in(base, 1), (pair_count,), 0, CAP - HPO + 1)
    forced = jax.random.randint(jax.random.fold_in(base, 2), (), 0, pair_count)
    spare = jnp.where(jnp.arange(pair_count, dtype=jnp.int32) == forced, 0, spare).astype(jnp.int32)
    totals = jnp.stack([CAP - spare, HPO + spare], axis=1).reshape(OWNERS).astype(jnp.int32)
    totals = jax.random.permutation(jax.random.fold_in(base, 3), totals)
    room = totals - HPO
    raw_cuts = jax.random.randint(jax.random.fold_in(base, 4), (OWNERS, HPO - 1), 0, CAP)
    cuts = jnp.sort(raw_cuts % (room[:, None] + 1), axis=1)
    cuts = jnp.where((totals == CAP)[:, None], room[:, None], cuts)
    edges = jnp.concatenate([jnp.zeros((OWNERS, 1), jnp.int32), cuts.astype(jnp.int32), room[:, None]], axis=1)
    parts = (edges[:, 1:] - edges[:, :-1] + 1).reshape(OWNERS * HPO).astype(jnp.int32)
    order = jax.random.permutation(jax.random.fold_in(base, 5), OWNERS * HPO)
    lengths = jnp.zeros((OWNERS * HPO,), jnp.int32).at[order].set(parts)
    owner_list = jnp.repeat(jnp.arange(OWNERS, dtype=jnp.int32), HPO)
    owner_of = jnp.zeros((OWNERS * HPO,), jnp.int32).at[order].set(owner_list)
    return (lengths, owner_of)


def draw_hist_len(key, part):
    return history_plan(key)[0]


def draw_hist_owner(key, part):
    return history_plan(key)[1]


def draw_item_table(key, part):
    base = jax.random.fold_in(key, 21)
    entries = jnp.clip(jax.random.normal(jax.random.fold_in(base, 1), (ITEMS, D), jnp.float32), -5.0, 5.0)
    return entries.astype(jnp.bfloat16)


def plant(values, key, low, high):
    place = [jax.random.randint(jax.random.fold_in(key, axis), (), 0, length) for axis, length in enumerate(values.shape)]
    main_axis = values.shape.index(max(values.shape))
    beside = place[:main_axis] + [(place[main_axis] + 1) % values.shape[main_axis]] + place[main_axis + 1:]
    return values.at[tuple(place)].set(low).at[tuple(beside)].set(high)


def block_levels(key, shape, cuts, smallest, top_value):
    loudness = 1.0
    for axis_at, shards_of in cuts:
        heights = jax.random.uniform(jax.random.fold_in(jax.random.fold_in(key, 6), axis_at), (shards_of,), jnp.float32, smallest / len(cuts), top_value / len(cuts))
        loudness = loudness * jnp.repeat(jnp.exp(heights), shape[axis_at] // shards_of).reshape((-1,) + (1,) * (len(shape) - 1 - axis_at))
    return loudness


def rank_bounds(number_of, skew):
    loads = [(1 << 20) // math.isqrt(grade ** skew) + 1 for grade in range(1, number_of + 1)]
    scale = 1 + sum(loads) // (1 << 30)
    return np.cumsum(np.array([max(1, weight // scale) for weight in loads]))


def ranked_ids(own_key, shape, number_of, skew):
    grid = rank_bounds(number_of, skew)
    ticket = jax.random.randint(jax.random.fold_in(own_key, 1), shape, 0, int(grid[number_of - 1]))
    standing = jnp.searchsorted(jnp.asarray(grid, jnp.int32), ticket, side="right")
    return jax.random.permutation(jax.random.fold_in(own_key, 2), number_of)[standing].astype(jnp.int32)


def bell_draw(stream_key, shape, width, most, shards=(), kind=jnp.bfloat16):
    drawn = width * jax.random.normal(stream_key, shape, jnp.float32)
    if shards:
        drawn = drawn * block_levels(stream_key, shape, shards, -0.22, 0.18)
    return jnp.clip(drawn, -most, most).astype(kind)


def setup_inputs(seed: int = 0) -> dict:
    splits = jax.random.split(jax.random.key(seed), 10)
    return {
        "item_ids": plant(ranked_ids(splits[0], (OWNERS, CAP), ITEMS, 2), jax.random.fold_in(splits[0], 3), 0, ITEMS - 1).astype(jnp.int32),
        "action_ids": plant(jax.random.randint(splits[1], (OWNERS, CAP), 0, ACTIONS), jax.random.fold_in(splits[1], 1), 0, ACTIONS - 1).astype(jnp.int32),
        "hist_len": draw_hist_len(jax.random.fold_in(splits[9], 71), 0),
        "hist_owner": draw_hist_owner(jax.random.fold_in(splits[9], 71), 0),
        "item_table": draw_item_table(jax.random.fold_in(splits[9], 71), 0),
        "action_table": bell_draw(splits[5], (ACTIONS, D), 1.0, 6.0, ((1, 8),)),
        "w_in": bell_draw(splits[6], (D, 4 * D), D ** -0.5, 0.1875),
        "w_out": bell_draw(splits[7], (D, D), D ** -0.5, 0.1875),
        "cotangent": bell_draw(splits[8], (OWNERS * CAP, D), 1.0, 6.0, ((0, 128),)),
    }


EPSILON = 1e-06

def layer_norm(values):
    centred = values - lax.optimization_barrier(jnp.mean(values, axis=-1, keepdims=True))
    spread = lax.optimization_barrier(jnp.mean(centred * centred, axis=-1, keepdims=True))
    return centred * lax.rsqrt(spread + EPSILON)

def slot_layout(hist_len, hist_owner, owner_index, slot_count):
    chosen = hist_owner == owner_index
    lengths = jnp.where(chosen, hist_len, 0).astype(jnp.int32)
    hist_ends = jnp.cumsum(lengths, dtype=jnp.int32)
    starts = (hist_ends - lengths).astype(jnp.int32)
    slot_index = jnp.arange(slot_count, dtype=jnp.int32)
    inside = chosen[None, :] & (starts[None, :] <= slot_index[:, None]) & (slot_index[:, None] < hist_ends[None, :])
    slot_start = lax.optimization_barrier(jnp.sum(jnp.where(inside, starts[None, :], 0), axis=1, dtype=jnp.int32))
    occupied = jnp.any(inside, axis=1)
    return (slot_start, occupied)

def mixer(pre_values, slot_start, occupied):
    row_count = pre_values.shape[0]
    activated = jax.nn.silu(pre_values).astype(jnp.bfloat16)
    gate_part, value_part, query_part, key_part = jnp.split(activated, 4, axis=1)
    queries = query_part.reshape(row_count, HEADS, HEAD).astype(jnp.float32)
    key_heads = key_part.reshape(row_count, HEADS, HEAD).astype(jnp.float32)
    scores = jnp.einsum('ihd,jhd->hij', queries, key_heads)
    positions = jnp.arange(row_count, dtype=jnp.int32)
    allowed = (positions[None, :] <= positions[:, None]) & (positions[None, :] >= slot_start[:, None]) & occupied[:, None]
    weights = jnp.where(allowed[None], jax.nn.silu(scores * HEAD ** (-0.5)) / CAP, 0.0).astype(jnp.bfloat16)
    value_heads = value_part.reshape(row_count, HEADS, HEAD).astype(jnp.float32)
    mixed_heads = jnp.einsum('hij,jhd->ihd', weights.astype(jnp.float32), value_heads).reshape(row_count, D)
    return layer_norm(mixed_heads) * gate_part.astype(jnp.float32)

def owner_pass(x_rows, grad_rows, slot_start, occupied, w_in, w_out):
    normed = layer_norm(x_rows.astype(jnp.float32)).astype(jnp.bfloat16)
    pre_act = jnp.dot(normed, w_in, preferred_element_type=jnp.float32)
    gated_f32, mixer_back = jax.vjp(lambda pre_values: mixer(pre_values, slot_start, occupied), pre_act)
    gated_rows = gated_f32.astype(jnp.bfloat16)
    result = (x_rows.astype(jnp.float32) + jnp.dot(gated_rows, w_out, preferred_element_type=jnp.float32)).astype(jnp.bfloat16)
    gated_grad = jnp.dot(grad_rows, w_out.T, preferred_element_type=jnp.float32).astype(jnp.bfloat16)
    pre_grad = mixer_back(gated_grad.astype(jnp.float32))[0].astype(jnp.bfloat16)
    normed_grad = jnp.dot(pre_grad, w_in.T, preferred_element_type=jnp.float32).astype(jnp.bfloat16)
    unused_value, norm_back = jax.vjp(layer_norm, x_rows.astype(jnp.float32))
    input_grad = (norm_back(normed_grad.astype(jnp.float32))[0] + grad_rows.astype(jnp.float32)) * occupied[:, None]
    in_grad = jnp.dot(normed.T, pre_grad, preferred_element_type=jnp.float32)
    out_grad = jnp.dot(gated_rows.T, grad_rows, preferred_element_type=jnp.float32)
    return (result, input_grad.astype(jnp.bfloat16), in_grad, out_grad)

def reference(item_ids, action_ids, hist_len, hist_owner, item_table, action_table, w_in, w_out, cotangent):
    owner_count = item_ids.shape[0]
    grads_all = cotangent.reshape(owner_count, CAP, D)

    def one_owner(totals, members):
        owner_items, owner_actions, grad_rows, owner_index = members
        slot_start, occupied = slot_layout(hist_len, hist_owner, owner_index, CAP)
        looked = item_table[owner_items].astype(jnp.float32) + action_table[owner_actions].astype(jnp.float32)
        x_rows = looked.astype(jnp.bfloat16) * occupied[:, None]
        result, input_grad, in_grad, out_grad = owner_pass(x_rows, grad_rows, slot_start, occupied, w_in, w_out)
        return ((totals[0] + in_grad, totals[1] + out_grad), (result, input_grad))
    initial = (jnp.zeros((D, 4 * D), jnp.float32), jnp.zeros((D, D), jnp.float32))
    owner_range = jnp.arange(owner_count, dtype=jnp.int32)
    sums, outputs = lax.scan(one_owner, initial, (item_ids, action_ids, grads_all, owner_range))
    results, input_grads = outputs
    return (results.reshape(owner_count * CAP, D), input_grads, sums[0] / owner_count, sums[1] / owner_count)
```

```python
import jax
import jax.numpy as jnp
from jax import lax
from jax.sharding import PartitionSpec as P

D = 1024
HEADS = 4
HEAD = 256
CAP = 512


EPSILON = 1e-06


def layer_norm(values):
    centred = values - jnp.mean(values, axis=-1, keepdims=True)
    spread = jnp.mean(centred * centred, axis=-1, keepdims=True)
    return centred * lax.rsqrt(spread + EPSILON)


def slot_layout(hist_len, hist_owner, owner_index, slot_count):
    chosen = hist_owner == owner_index
    lengths = jnp.where(chosen, hist_len, 0)
    hist_ends = jnp.cumsum(lengths, dtype=jnp.int32)
    starts = hist_ends - lengths
    slot_index = jnp.arange(slot_count, dtype=jnp.int32)
    inside = (
        chosen[None, :]
        & (starts[None, :] <= slot_index[:, None])
        & (slot_index[:, None] < hist_ends[None, :])
    )
    slot_start = jnp.sum(jnp.where(inside, starts[None, :], 0), axis=1, dtype=jnp.int32)
    occupied = jnp.any(inside, axis=1)
    return (slot_start, occupied)


def mixer(pre_values, slot_start, occupied):
    row_count = pre_values.shape[0]
    activated = jax.nn.silu(pre_values).astype(jnp.bfloat16)
    gate_part, value_part, query_part, key_part = jnp.split(activated, 4, axis=1)
    queries = query_part.reshape(row_count, HEADS, HEAD)
    key_heads = key_part.reshape(row_count, HEADS, HEAD)
    scores = jnp.einsum("ihd,jhd->hij", queries, key_heads, preferred_element_type=jnp.float32)
    positions = jnp.arange(row_count, dtype=jnp.int32)
    allowed = (
        (positions[None, :] <= positions[:, None])
        & (positions[None, :] >= slot_start[:, None])
        & occupied[:, None]
    )
    weights = jnp.where(allowed[None], jax.nn.silu(scores * HEAD ** (-0.5)) / CAP, 0.0).astype(
        jnp.bfloat16
    )
    value_heads = value_part.reshape(row_count, HEADS, HEAD)
    mixed_heads = jnp.einsum(
        "hij,jhd->ihd", weights, value_heads, preferred_element_type=jnp.float32
    ).reshape(row_count, D)
    return layer_norm(mixed_heads) * gate_part.astype(jnp.float32)


def local_pass(x_rows, grad_rows, slot_start, occupied, w_in, w_out):
    normed = layer_norm(x_rows.astype(jnp.float32)).astype(jnp.bfloat16)
    pre_act = jnp.dot(normed, w_in, preferred_element_type=jnp.float32)
    gated_f32, mixer_back = jax.vjp(
        lambda pre_values: mixer(pre_values, slot_start, occupied), pre_act
    )
    gated_rows = gated_f32.astype(jnp.bfloat16)
    result = (
        x_rows.astype(jnp.float32) + jnp.dot(gated_rows, w_out, preferred_element_type=jnp.float32)
    ).astype(jnp.bfloat16)
    gated_grad = jnp.dot(grad_rows, w_out.T, preferred_element_type=jnp.float32).astype(
        jnp.bfloat16
    )
    pre_grad = mixer_back(gated_grad.astype(jnp.float32))[0].astype(jnp.bfloat16)
    normed_grad = jnp.dot(pre_grad, w_in.T, preferred_element_type=jnp.float32).astype(jnp.bfloat16)
    unused_value, norm_back = jax.vjp(layer_norm, x_rows.astype(jnp.float32))
    input_grad = (
        norm_back(normed_grad.astype(jnp.float32))[0] + grad_rows.astype(jnp.float32)
    ) * occupied[:, None]
    return (result, input_grad.astype(jnp.bfloat16), normed, pre_grad, gated_rows)


def device_pairs(partner):
    pairs = []
    for device in range(128):
        emb, seq = divmod(device, 16)
        y, core, x, z = partner(emb // 2, emb % 2, seq // 4, seq % 4)
        pairs.append((device, (2 * y + core) * 16 + 4 * x + z))
    return pairs


CORE_PAIRS = device_pairs(lambda y, c, x, z: (y, 1 - c, x, z))
AXIS_PAIRS = {
    "y1": device_pairs(lambda y, c, x, z: (3 - y, c, x, z)),
    "y0": device_pairs(lambda y, c, x, z: (y ^ 1, c, x, z)),
    "x1": device_pairs(lambda y, c, x, z: (y, c, 3 - x, z)),
    "x0": device_pairs(lambda y, c, x, z: (y, c, x ^ 1, z)),
    "z1": device_pairs(lambda y, c, x, z: (y, c, x, 3 - z)),
    "z0": device_pairs(lambda y, c, x, z: (y, c, x, z ^ 1)),
}
BITS = ("y1", "y0", "x1", "x0", "z1", "z0")


def half(values, dim, which):
    return lax.dynamic_slice_in_dim(values, which, 1, axis=dim)


def halving_sum(kept, arrived, order, bits):
    for name in order:
        dim, own = BITS.index(name), bits[name]
        outgoing = (
            half(kept, dim, 1 - own) + half(arrived, dim, 1 - own).astype(jnp.float32)
        ).astype(jnp.bfloat16)
        kept = half(kept, dim, own) + half(arrived, dim, own).astype(jnp.float32)
        arrived = lax.ppermute(outgoing, ("emb", "seq"), AXIS_PAIRS[name])
    return (kept + arrived.astype(jnp.float32)).reshape(8, -1)


def weight_grads(normed, pre_grad, gated_rows, cotangent):
    emb, seq = lax.axis_index("emb"), lax.axis_index("seq")
    core = emb % 2
    bits = {
        "y1": emb // 4, "y0": emb // 2 % 2,
        "x1": seq // 8, "x0": seq // 4 % 2, "z1": seq // 2 % 2, "z0": seq % 2,
    }

    def rows_of(values, which):
        return half(values.reshape(-1, 4, 2, 128), 2, which).reshape(-1, 512)

    def grads(which):
        lhs_in, lhs_out = rows_of(normed, which), rows_of(gated_rows, which)
        in_part = lax.dot_general(lhs_in, pre_grad, (((0,), (0,)), ((), ())), preferred_element_type=jnp.float32)
        out_part = lax.dot_general(lhs_out, cotangent, (((0,), (0,)), ((), ())), preferred_element_type=jnp.float32)
        parts = (
            in_part[:, :1664],
            in_part[:, 1664:3328],
            jnp.concatenate([in_part[:, 3328:], out_part], axis=1),
        )
        return [part.reshape(2, 2, 2, 2, 2, 2, 8, -1) for part in parts]

    outgoing = [part.astype(jnp.bfloat16) for part in grads(1 - core)]
    arrived = [lax.ppermute(part, ("emb", "seq"), CORE_PAIRS) for part in outgoing]
    kept = grads(core)
    orders = (
        ("y1", "y0", "x1", "x0", "z1", "z0"),
        ("x1", "x0", "z1", "z0", "y1", "y0"),
        ("z1", "z0", "y1", "y0", "x1", "x0"),
    )
    sums = [halving_sum(k, a, order, bits) for k, a, order in zip(kept, arrived, orders)]
    in_share = jnp.concatenate([sums[0], sums[1], sums[2][:, :768]], axis=1)
    return in_share, sums[2][:, 768:]


def shards(
    item_ids, action_ids, hist_len, hist_owner, item_table, action_table, w_in, w_out, cotangent
):
    emb_count = lax.axis_size("emb")
    seq_count = lax.axis_size("seq")
    device_count = emb_count * seq_count
    owner_count = item_ids.shape[0]
    slot_rows = item_ids.shape[1]
    column_width = item_table.shape[1]
    looked_items = jnp.take(item_table, item_ids, axis=0).astype(jnp.float32)
    action_hot = (
        action_ids[:, :, None] == jnp.arange(action_table.shape[0], dtype=jnp.int32)
    ).astype(jnp.bfloat16)
    looked_actions = jnp.einsum(
        "osa,ac->osc", action_hot, action_table, preferred_element_type=jnp.float32
    )
    looked = (looked_items + looked_actions).astype(jnp.bfloat16)
    arrived = lax.all_to_all(looked, ("emb", "seq"), split_axis=0, concat_axis=0, tiled=True)
    x_rows = (
        arrived.reshape(emb_count, seq_count, slot_rows, column_width)
        .transpose(1, 2, 0, 3)
        .reshape(seq_count * slot_rows, emb_count * column_width)
    )
    owner_index = lax.axis_index(("emb", "seq"))
    slot_start, occupied = slot_layout(hist_len, hist_owner, owner_index, x_rows.shape[0])
    x_rows = x_rows * occupied[:, None]
    result, input_grad, normed, pre_grad, gated_rows = local_pass(
        x_rows, cotangent, slot_start, occupied, w_in, w_out
    )
    outgoing = (
        input_grad.reshape(seq_count, slot_rows, emb_count, column_width)
        .transpose(2, 0, 1, 3)
        .reshape(owner_count, slot_rows, column_width)
    )
    row_grads = lax.all_to_all(outgoing, ("emb", "seq"), split_axis=0, concat_axis=0, tiled=True)
    in_share, out_share = weight_grads(normed, pre_grad, gated_rows, cotangent)
    return (result, row_grads, in_share / device_count, out_share / device_count)


def solution(mesh):
    in_specs = (
        P(None, "seq"),
        P(None, "seq"),
        P(),
        P(),
        P(None, "emb"),
        P(None, "emb"),
        P(),
        P(),
        P(("emb", "seq"), None),
    )
    out_specs = (
        P(("emb", "seq"), None),
        P(None, "seq", "emb"),
        P(("emb", "seq"), None),
        P(("emb", "seq"), None),
    )
    return jax.shard_map(shards, mesh=mesh, in_specs=in_specs, out_specs=out_specs, check_vma=False)
```

```python
import jax
import jax.numpy as jnp
from jax import lax
from jax.experimental import pallas as pl
from jax.experimental.pallas import tpu as pltpu
from jax.sharding import PartitionSpec as P

D = 1024
HEADS = 4
HEAD = 256
CAP = 512


EPSILON = 1e-06


def slot_layout(hist_len, hist_owner, owner_index, slot_count):
    chosen = hist_owner == owner_index
    lengths = jnp.where(chosen, hist_len, 0)
    hist_ends = jnp.cumsum(lengths, dtype=jnp.int32)
    starts = hist_ends - lengths
    slot_index = jnp.arange(slot_count, dtype=jnp.int32)
    inside = (
        chosen[None, :]
        & (starts[None, :] <= slot_index[:, None])
        & (slot_index[:, None] < hist_ends[None, :])
    )
    slot_start = jnp.sum(jnp.where(inside, starts[None, :], 0), axis=1, dtype=jnp.int32)
    occupied = jnp.any(inside, axis=1)
    return (slot_start, occupied)


F32, BF16 = jnp.float32, jnp.bfloat16
TILE = 256
CUTS = ((0, 1792), (1792, 3584), (3584, 5120))
ROWS = 128


def mm(a, b):
    return jnp.dot(a, b, preferred_element_type=F32)


def mm_nt(a, b):
    return lax.dot_general(a, b, (((1,), (1,)), ((), ())), preferred_element_type=F32)


def mm_tn(a, b):
    return lax.dot_general(a, b, (((0,), (0,)), ((), ())), preferred_element_type=F32)


def silu_pair(v):
    sig = 0.5 * jnp.tanh(0.5 * v) + 0.5
    act = v * sig
    return act, sig + act * (1.0 - sig)


def normalise(v):
    mean = jnp.mean(v, axis=-1, keepdims=True)
    centred = v - mean
    spread = jnp.mean(centred * centred, axis=-1, keepdims=True)
    rstd = lax.rsqrt(spread + EPSILON)
    return centred * rstd, rstd


def norm_grad(g, hat, rstd):
    return rstd * (
        g - jnp.mean(g, axis=-1, keepdims=True) - hat * jnp.mean(g * hat, axis=-1, keepdims=True)
    )


def tile_at(t):
    return pl.ds(pl.multiple_of(t * TILE, TILE), TILE)


def rows_at(r):
    return pl.ds(pl.multiple_of(r * ROWS, ROWS), ROWS)


def layer_kernel(
    core_ref, arrived_ref, first_ref, cot_ref, w_in_ref, gg_in, w_out_in,
    row_grad_ref, hist_out, send_y, send_x, send_z, keep_y, keep_x, keep_z,
    w_out_ref, gg_ref, x_ref, hist_ref, pre_grad_ref, turned_ref, gated_turned_ref,
    normed_ref, act_ref, der_ref, wts_ref, wder_ref, mixed_ref, gated_ref, dmix_ref, ds_ref,
    pre_a_ref, pre_b_ref, grads_ref, in_sems, out_sems,
):
    core = core_ref[0]
    gg_load = pltpu.make_async_copy(gg_in, gg_ref, in_sems.at[0])
    w_out_load = pltpu.make_async_copy(w_out_in, w_out_ref, in_sems.at[1])
    gg_load.start()
    w_out_load.start()
    stores = []

    def store(src, dst):
        copy = pltpu.make_async_copy(src, dst, out_sems.at[len(stores)])
        copy.start()
        stores.append(copy)

    def turn(src, dst, k):
        for r in range(CAP // ROWS):
            rows = slice(r * ROWS, (r + 1) * ROWS)
            dst[k, :, rows] = src[rows, pl.ds(pl.multiple_of(128 * k, 128), 128)].T

    def embed():
        @pl.loop(0, CAP // ROWS)
        def _(r):
            rows = rows_at(r)
            x = jnp.concatenate(
                [arrived_ref[e, pl.ds(4 * r, 4)].reshape(ROWS, 128) for e in range(8)], axis=1
            ).astype(F32)
            x = jnp.where(first_ref[rows, :] < CAP, x, 0.0)
            x_ref[rows, :] = x.astype(BF16)
            normed_ref[rows, :] = normalise(x)[0].astype(BF16)

    def project():
        def multiply(into, t):
            into[...] = mm(normed_ref[...], w_in_ref[:, tile_at(t)])

        def activate(pre, t):
            act, der = silu_pair(pre[...])
            act_ref[:, tile_at(t)] = act.astype(BF16)
            der_ref[:, tile_at(t)] = der.astype(BF16)

        multiply(pre_a_ref, 0)

        @pl.loop(0, 7)
        def _(u):
            multiply(pre_b_ref, 2 * u + 1)
            activate(pre_a_ref, 2 * u)
            turn(normed_ref, turned_ref, u)
            multiply(pre_a_ref, 2 * u + 2)
            activate(pre_b_ref, 2 * u + 1)

        multiply(pre_b_ref, 15)
        activate(pre_a_ref, 14)
        turn(normed_ref, turned_ref, 7)
        activate(pre_b_ref, 15)

    def attend():
        @pl.loop(0, HEADS)
        def _(h):
            for i in range(2):
                rows, seen = slice(i * 256, i * 256 + 256), (i + 1) * 256
                v = act_ref[0:seen, tile_at(h + 4)]
                q = act_ref[rows, tile_at(h + 8)]
                k = act_ref[0:seen, tile_at(h + 12)]
                act, der = silu_pair(mm_nt(q, k) * HEAD**-0.5)
                at = lax.broadcasted_iota(jnp.int32, (256, seen), 0) + i * 256
                of = lax.broadcasted_iota(jnp.int32, (256, seen), 1)
                allowed = (of <= at) & (of >= first_ref[rows, :])
                wts = jnp.where(allowed, act * (1.0 / CAP), 0.0).astype(BF16)
                wts_ref[h, rows, 0:seen] = wts
                wder_ref[h, rows, 0:seen] = jnp.where(
                    allowed, der * (HEAD**-0.5 / CAP), 0.0
                ).astype(BF16)
                mixed_ref[rows, tile_at(h)] = mm(wts, v)

    def mix():
        gg_load.wait()

        @pl.loop(0, CAP // ROWS)
        def _(r):
            rows = rows_at(r)
            hat, rstd = normalise(mixed_ref[rows, :])
            gate = act_ref[rows, 0:D].astype(F32)
            gg = gg_ref[rows, :].astype(F32)
            gated_ref[rows, :] = (hat * gate).astype(BF16)
            pre_grad_ref[rows, 0:D] = (
                (gg * hat).astype(BF16).astype(F32) * der_ref[rows, 0:D].astype(F32)
            ).astype(BF16)
            dmix_ref[rows, :] = norm_grad(gg * gate, hat, rstd).astype(BF16)

    def finish():
        w_out_load.wait()

        @pl.loop(0, 4)
        def _(t):
            hist_ref[:, tile_at(t)] = (
                x_ref[:, tile_at(t)].astype(F32) + mm(gated_ref[...], w_out_ref[:, tile_at(t)])
            ).astype(BF16)
            turn(gated_ref, gated_turned_ref, 2 * t)
            turn(gated_ref, gated_turned_ref, 2 * t + 1)

        store(hist_ref, hist_out)

    def put(rows, t, grad):
        pre_grad_ref[rows, tile_at(t)] = (
            grad.astype(BF16).astype(F32) * der_ref[rows, tile_at(t)].astype(F32)
        ).astype(BF16)

    def back():
        @pl.loop(0, HEADS)
        def _(h):
            for i in range(2):
                rows, seen = slice(i * 256, i * 256 + 256), (i + 1) * 256
                dmix = dmix_ref[rows, tile_at(h)]
                dw = mm_nt(dmix, act_ref[0:seen, tile_at(h + 4)]).astype(BF16).astype(F32)
                ds = (dw * wder_ref[h, rows, 0:seen].astype(F32)).astype(BF16)
                ds_ref[rows, 0:seen] = ds
                put(rows, h + 8, mm(ds, act_ref[0:seen, tile_at(h + 12)]))
            for j in range(2):
                cols, below = slice(j * 256, j * 256 + 256), slice(j * 256, CAP)
                put(cols, h + 4, mm_tn(wts_ref[h, below, cols], dmix_ref[below, tile_at(h)]))
                put(cols, h + 12, mm_tn(ds_ref[below, cols], act_ref[below, tile_at(h + 8)]))

    def weight_grads():
        def put_grads(turned, right, t, at):
            sums = mm(turned[...].reshape(D, CAP), right[:, tile_at(t)]).astype(BF16)
            for k in range(8):
                grads_ref[k % 2, 128 * (k // 2) : 128 * (k // 2) + 128, tile_at(t + at)] = sums[
                    128 * k : 128 * k + 128
                ]

        @pl.loop(0, 4)
        def _(t):
            put_grads(gated_turned_ref, cot_ref, t, 16)

        @pl.loop(0, 16)
        def _(t):
            put_grads(turned_ref, pre_grad_ref, t, 0)

        outs = ((send_y, keep_y), (send_x, keep_x), (send_z, keep_z))
        for (low, high), (send, keep) in zip(CUTS, outs):
            store(grads_ref.at[1 - core, :, low:high], send)
            store(grads_ref.at[core, :, low:high], keep)

    def row_grads():
        @pl.loop(0, 4)
        def _(t):
            gated_ref[:, tile_at(t)] = mm_nt(pre_grad_ref[...], w_in_ref[tile_at(t), :]).astype(BF16)

        @pl.loop(0, CAP // ROWS)
        def _(r):
            rows = rows_at(r)
            hat, rstd = normalise(x_ref[rows, :].astype(F32))
            grad = norm_grad(gated_ref[rows, :].astype(F32), hat, rstd) + cot_ref[rows, :].astype(F32)
            grad = jnp.where(first_ref[rows, :] < CAP, grad, 0.0).astype(BF16)
            for e in range(8):
                row_grad_ref[e, pl.ds(4 * r, 4)] = grad[:, 128 * e : 128 * e + 128].reshape(4, 32, 128)

    embed()
    project()
    attend()
    mix()
    finish()
    back()
    weight_grads()
    row_grads()
    for copy in stores:
        copy.wait()


def lookup_kernel(items_ref, actions_ref, table_in, action_in, out_ref, table_ref, wide_ref, action_ref, rows_ref, sems):
    pieces = 8
    size = table_ref.shape[0] // pieces

    def load(n):
        rows = pl.ds(pl.multiple_of(n * size, size), size)
        return pltpu.make_async_copy(table_in.at[rows, :], table_ref.at[rows, :], sems.at[n])

    for n in range(pieces):
        load(n).start()
    action_ref[...] = action_in[...].astype(F32)

    @pl.loop(0, pieces)
    def _(n):
        load(n).wait()

        @pl.loop(0, size // 256)
        def _(k):
            rows = pl.ds(pl.multiple_of(n * size + k * 256, 256), 256)
            wide_ref[rows, :] = table_ref[rows, :].astype(F32)

    slots, owners = items_ref.shape

    @pl.loop(0, owners)
    def _(owner):
        for slot in range(slots):
            rows_ref[pl.ds(owner * slots + slot, 1), :] = (
                wide_ref[pl.ds(items_ref[slot, owner], 1), :]
                + action_ref[pl.ds(actions_ref[slot, owner], 1), :]
            )

    @pl.loop(0, owners // 8)
    def _(k):
        rows = pl.ds(pl.multiple_of(k * 8 * slots, 256), 8 * slots)
        out_ref[pl.ds(k * 8, 8)] = rows_ref[rows, :].astype(BF16).reshape(8, slots, 128)


def run_lookup(item_ids, action_ids, item_table, action_table):
    owners, slots = item_ids.shape
    return pl.pallas_call(
        lookup_kernel,
        out_shape=jax.ShapeDtypeStruct((owners, slots, 128), BF16),
        in_specs=[SMEM, SMEM, ANYWHERE, VMEM],
        out_specs=VMEM,
        scratch_shapes=[
            pltpu.VMEM(item_table.shape, BF16),
            pltpu.VMEM(item_table.shape, F32),
            pltpu.VMEM(action_table.shape, F32),
            pltpu.VMEM((owners * slots, 128), F32),
            pltpu.SemaphoreType.DMA((8,)),
        ],
        compiler_params=pltpu.CompilerParams(vmem_limit_bytes=58 << 20),
    )(item_ids.T, action_ids.T, item_table, action_table)


def run_layer(core, arrived, first, cotangent, gated_grad, w_in, w_out):
    part, whole = (CAP, D), (CAP, 4 * D)
    turned, square = (8, 128, CAP), (HEADS, CAP, CAP)
    scratch = [
        (w_out.shape, BF16), (part, BF16), (part, BF16), (part, BF16), (whole, BF16),
        (turned, BF16), (turned, BF16), (part, BF16), (whole, BF16), (whole, BF16), (square, BF16),
        (square, BF16), (part, F32), (part, BF16), (part, BF16), ((CAP, CAP), BF16),
        ((CAP, TILE), F32), ((CAP, TILE), F32), ((2, 512, 5 * D), BF16),
    ]
    return pl.pallas_call(
        layer_kernel,
        out_shape=[
            jax.ShapeDtypeStruct(shape, BF16)
            for shape in [arrived.shape, part] + 2 * [(512, high - low) for low, high in CUTS]
        ],
        in_specs=[SMEM, VMEM, VMEM, VMEM, VMEM, ANYWHERE, ANYWHERE],
        out_specs=[VMEM] + [ANYWHERE] * 7,
        scratch_shapes=[pltpu.VMEM(*one) for one in scratch]
        + [
            pltpu.SemaphoreType.DMA((2,)),
            pltpu.SemaphoreType.DMA((9,)),
        ],
        cost_estimate=pl.CostEstimate(
            flops=18_000_000_000, bytes_accessed=26 << 20, transcendentals=0
        ),
        compiler_params=pltpu.CompilerParams(vmem_limit_bytes=54 << 20),
    )(core, arrived, first, cotangent, w_in, gated_grad, w_out)


ANYWHERE = pl.BlockSpec(memory_space=pl.ANY)
VMEM = pl.BlockSpec(memory_space=pltpu.VMEM)
SMEM = pl.BlockSpec(memory_space=pltpu.SMEM)


def device_pairs(partner):
    pairs = []
    for device in range(128):
        emb, seq = divmod(device, 16)
        y, core, x, z = partner(emb // 2, emb % 2, seq // 4, seq % 4)
        pairs.append((device, (2 * y + core) * 16 + 4 * x + z))
    return pairs


CORE_PAIRS = device_pairs(lambda y, c, x, z: (y, 1 - c, x, z))
AXIS_PAIRS = {
    "y1": device_pairs(lambda y, c, x, z: (3 - y, c, x, z)),
    "x1": device_pairs(lambda y, c, x, z: (y, c, 3 - x, z)),
    "z1": device_pairs(lambda y, c, x, z: (y, c, x, 3 - z)),
}
BITS = ("y1", "y0", "x1", "x0", "z1", "z0")


def half(values, dim, which):
    return lax.dynamic_slice_in_dim(values, which, 1, axis=dim)


ORDERS = (("y1", "x1", "z1"), ("x1", "z1", "y1"), ("z1", "y1", "x1"))


def cubes():
    found = {}
    for device in range(128):
        emb, seq = divmod(device, 16)
        y, core, x, z = emb // 2, emb % 2, seq // 4, seq % 4
        found.setdefault((y // 2, core, x // 2, z // 2), []).append((y % 2, x % 2, z % 2, device))
    return [[member[3] for member in sorted(cube)] for cube in found.values()]


def add(a, b):
    return a.astype(F32) + b.astype(F32)


def copy_kernel(in_ref, out_ref):
    out_ref[...] = in_ref[...]


def copy_out(values):
    return pl.pallas_call(
        copy_kernel,
        grid=(4,),
        out_shape=jax.ShapeDtypeStruct(values.shape, values.dtype),
        in_specs=[pl.BlockSpec((32, 32, 128), lambda k: (k, 0, 0))],
        out_specs=pl.BlockSpec((32, 32, 128), lambda k: (k, 0, 0)),
    )(values)


def chip_sums(keep, got, bits, meanwhile):
    keeps = [v.reshape(2, 2, 2, 2, 2, 2, 8, -1) for v in keep]
    arrived = [v.reshape(2, 2, 2, 2, 2, 2, 8, -1) for v in got]
    for step in range(3):
        for p, order in enumerate(ORDERS):
            name = order[step]
            dim, own = BITS.index(name), bits[name]
            outgoing = add(half(keeps[p], dim, 1 - own), half(arrived[p], dim, 1 - own)).astype(BF16)
            keeps[p] = add(half(keeps[p], dim, own), half(arrived[p], dim, own))
            if step == 0:
                keeps[p] = keeps[p].astype(BF16)
            arrived[p] = lax.ppermute(outgoing, ("emb", "seq"), AXIS_PAIRS[name])
        if step == 0:
            *arrived, meanwhile = lax.optimization_barrier((*arrived, meanwhile))
            meanwhile = copy_out(meanwhile)
        if step == 1:
            *arrived, meanwhile = lax.optimization_barrier((*arrived, meanwhile))
    total = jnp.concatenate(
        [add(keeps[p], arrived[p]).astype(BF16).reshape(8, 8, -1) for p in range(3)], axis=2
    )
    total = lax.all_to_all(total, ("emb", "seq"), 0, 0, tiled=True, axis_index_groups=cubes())
    return jnp.sum(total.astype(F32), axis=0), meanwhile


def shards(
    item_ids, action_ids, hist_len, hist_owner, item_table, action_table, w_in, w_out, cotangent
):
    emb_count = lax.axis_size("emb")
    seq_count = lax.axis_size("seq")
    device_count = emb_count * seq_count
    owner_count = item_ids.shape[0]
    slot_rows = item_ids.shape[1]
    column_width = item_table.shape[1]
    looked = run_lookup(item_ids, action_ids, item_table, action_table)
    arrived = lax.all_to_all(looked, ("emb", "seq"), split_axis=0, concat_axis=0, tiled=True)
    arrived = arrived.reshape(emb_count, seq_count, slot_rows, column_width)
    owner_index = lax.axis_index(("emb", "seq"))
    slot_start, occupied = slot_layout(hist_len, hist_owner, owner_index, CAP)
    first = jnp.where(occupied, slot_start, CAP).astype(jnp.int32)[:, None]
    emb, seq = lax.axis_index("emb"), lax.axis_index("seq")
    bits = {
        "y1": emb // 4, "y0": emb // 2 % 2,
        "x1": seq // 8, "x0": seq // 4 % 2, "z1": seq // 2 % 2, "z0": seq % 2,
    }
    core = (emb % 2).astype(jnp.int32).reshape(1)
    gated_grad = mm_nt(cotangent, w_out).astype(BF16)
    outgoing, result, *grads = run_layer(
        core, arrived, first, cotangent, gated_grad, w_in, w_out
    )
    got = [lax.ppermute(send, ("emb", "seq"), CORE_PAIRS) for send in grads[:3]]
    outgoing = outgoing.reshape(owner_count, slot_rows, column_width)
    row_grads = lax.all_to_all(outgoing, ("emb", "seq"), split_axis=0, concat_axis=0, tiled=True)
    sums, row_grads = chip_sums(grads[3:], got, bits, row_grads)
    in_share, out_share = sums[:, : 4 * D], sums[:, 4 * D :]
    return (result, row_grads, in_share / device_count, out_share / device_count)


def solution(mesh):
    in_specs = (
        P(None, "seq"),
        P(None, "seq"),
        P(),
        P(),
        P(None, "emb"),
        P(None, "emb"),
        P(),
        P(),
        P(("emb", "seq"), None),
    )
    out_specs = (
        P(("emb", "seq"), None),
        P(None, "seq", "emb"),
        P(("emb", "seq"), None),
        P(("emb", "seq"), None),
    )
    return jax.shard_map(shards, mesh=mesh, in_specs=in_specs, out_specs=out_specs, check_vma=False)
```

```python
import functools

import jax
import jax.numpy as jnp
from jax import lax
from jax.experimental import pallas as pl
from jax.experimental.pallas import tpu as pltpu
from jax.sharding import PartitionSpec as P

D = 1024
HEADS = 4
HEAD = 256
CAP = 512


EPSILON = 1e-06


def slot_layout(hist_len, hist_owner, owner_index, slot_count):
    chosen = hist_owner == owner_index
    lengths = jnp.where(chosen, hist_len, 0)
    hist_ends = jnp.cumsum(lengths, dtype=jnp.int32)
    starts = hist_ends - lengths
    slot_index = jnp.arange(slot_count, dtype=jnp.int32)
    inside = (
        chosen[None, :]
        & (starts[None, :] <= slot_index[:, None])
        & (slot_index[:, None] < hist_ends[None, :])
    )
    slot_start = jnp.sum(jnp.where(inside, starts[None, :], 0), axis=1, dtype=jnp.int32)
    occupied = jnp.any(inside, axis=1)
    return (slot_start, occupied)


F32, BF16 = jnp.float32, jnp.bfloat16
TILE = 256
CUTS = ((0, 1792), (1792, 3584), (3584, 5120))
ROWS = 256


def mm(a, b):
    return jnp.dot(a, b, preferred_element_type=F32)


def mm_nt(a, b):
    return lax.dot_general(a, b, (((1,), (1,)), ((), ())), preferred_element_type=F32)


def mm_tn(a, b):
    return lax.dot_general(a, b, (((0,), (0,)), ((), ())), preferred_element_type=F32)


def silu_pair(v):
    sig = 0.5 * jnp.tanh(0.5 * v) + 0.5
    act = v * sig
    return act, sig + act * (1.0 - sig)


def normalise(v):
    mean = jnp.mean(v, axis=-1, keepdims=True)
    centred = v - mean
    spread = jnp.mean(centred * centred, axis=-1, keepdims=True)
    rstd = lax.rsqrt(spread + EPSILON)
    return centred * rstd, rstd


def norm_grad(g, hat, rstd):
    return rstd * (
        g - jnp.mean(g, axis=-1, keepdims=True) - hat * jnp.mean(g * hat, axis=-1, keepdims=True)
    )


def tile_at(t):
    return pl.ds(pl.multiple_of(t * TILE, TILE), TILE)


def rows_at(r):
    return pl.ds(pl.multiple_of(r * ROWS, ROWS), ROWS)


def layer_kernel(
    core_ref, arrived_ref, first_ref, cot_ref, w_in_ref, gg_in, w_out_in,
    row_grad_ref, hist_out, turned_out, gated_turned_out, grad_y_out, grad_x_out, grad_z_out,
    w_out_ref, gg_ref, x_ref, hist_ref, pre_grad_ref, turned_ref, gated_turned_ref,
    normed_ref, act_ref, der_ref, wts_ref, wder_ref, mixed_ref, gated_ref, dmix_ref, ds_ref,
    pre_a_ref, pre_b_ref, in_sems, out_sems,
):
    core = core_ref[0]
    gg_load = pltpu.make_async_copy(gg_in, gg_ref, in_sems.at[0])
    w_out_load = pltpu.make_async_copy(w_out_in, w_out_ref, in_sems.at[1])
    gg_load.start()
    w_out_load.start()
    stores = []

    def store(src, dst):
        copy = pltpu.make_async_copy(src, dst, out_sems.at[len(stores)])
        copy.start()
        stores.append(copy)

    def turn(src, dst, k):
        for r in range(4):
            rows = slice(r * 128, r * 128 + 128)
            dst[k, :, rows] = src[rows, pl.ds(pl.multiple_of(128 * k, 128), 128)].T

    def embed():
        @pl.loop(0, CAP // ROWS)
        def _(r):
            rows = rows_at(r)
            x = jnp.concatenate(
                [arrived_ref[e, pl.ds(8 * r, 8)].reshape(ROWS, 128) for e in range(8)], axis=1
            ).astype(F32)
            x = jnp.where(first_ref[rows, :] < CAP, x, 0.0)
            x_ref[rows, :] = x.astype(BF16)
            normed_ref[rows, :] = normalise(x)[0].astype(BF16)

    def project():
        def multiply(into, t):
            into[...] = mm(normed_ref[...], w_in_ref[:, tile_at(t)])

        def activate(pre, t):
            act, der = silu_pair(pre[...])
            act_ref[:, tile_at(t)] = act.astype(BF16)
            der_ref[:, tile_at(t)] = der.astype(BF16)

        multiply(pre_a_ref, 0)

        @pl.loop(0, 7)
        def _(u):
            multiply(pre_b_ref, 2 * u + 1)
            activate(pre_a_ref, 2 * u)
            turn(normed_ref, turned_ref, u)
            multiply(pre_a_ref, 2 * u + 2)
            activate(pre_b_ref, 2 * u + 1)

        multiply(pre_b_ref, 15)
        activate(pre_a_ref, 14)
        turn(normed_ref, turned_ref, 7)
        activate(pre_b_ref, 15)

    def attend():
        @pl.loop(0, HEADS)
        def _(h):
            for i in range(2):
                rows, seen = slice(i * 256, i * 256 + 256), (i + 1) * 256
                v = act_ref[0:seen, tile_at(h + 4)]
                q = act_ref[rows, tile_at(h + 8)]
                k = act_ref[0:seen, tile_at(h + 12)]
                act, der = silu_pair(mm_nt(q, k) * HEAD**-0.5)
                at = lax.broadcasted_iota(jnp.int32, (256, seen), 0) + i * 256
                of = lax.broadcasted_iota(jnp.int32, (256, seen), 1)
                allowed = (of <= at) & (of >= first_ref[rows, :])
                wts = jnp.where(allowed, act * (1.0 / CAP), 0.0).astype(BF16)
                wts_ref[h, rows, 0:seen] = wts
                wder_ref[h, rows, 0:seen] = jnp.where(
                    allowed, der * (HEAD**-0.5 / CAP), 0.0
                ).astype(BF16)
                mixed_ref[rows, tile_at(h)] = mm(wts, v)

    def mix():
        gg_load.wait()

        @pl.loop(0, CAP // ROWS)
        def _(r):
            rows = rows_at(r)
            hat, rstd = normalise(mixed_ref[rows, :])
            gate = act_ref[rows, 0:D].astype(F32)
            gg = gg_ref[rows, :].astype(F32)
            gated_ref[rows, :] = (hat * gate).astype(BF16)
            pre_grad_ref[rows, 0:D] = (
                (gg * hat).astype(BF16).astype(F32) * der_ref[rows, 0:D].astype(F32)
            ).astype(BF16)
            dmix_ref[rows, :] = norm_grad(gg * gate, hat, rstd).astype(BF16)

    def finish():
        w_out_load.wait()

        @pl.loop(0, 4)
        def _(t):
            hist_ref[:, tile_at(t)] = (
                x_ref[:, tile_at(t)].astype(F32) + mm(gated_ref[...], w_out_ref[:, tile_at(t)])
            ).astype(BF16)
            turn(gated_ref, gated_turned_ref, 2 * t)
            turn(gated_ref, gated_turned_ref, 2 * t + 1)

        store(hist_ref, hist_out)
        store(turned_ref, turned_out)
        store(gated_turned_ref, gated_turned_out)

    def put(rows, t, grad):
        pre_grad_ref[rows, tile_at(t)] = (
            grad.astype(BF16).astype(F32) * der_ref[rows, tile_at(t)].astype(F32)
        ).astype(BF16)

    def back():
        @pl.loop(0, HEADS)
        def _(h):
            for i in range(2):
                rows, seen = slice(i * 256, i * 256 + 256), (i + 1) * 256
                dmix = dmix_ref[rows, tile_at(h)]
                dw = mm_nt(dmix, act_ref[0:seen, tile_at(h + 4)]).astype(BF16).astype(F32)
                ds = (dw * wder_ref[h, rows, 0:seen].astype(F32)).astype(BF16)
                ds_ref[rows, 0:seen] = ds
                put(rows, h + 8, mm(ds, act_ref[0:seen, tile_at(h + 12)]))
            for j in range(2):
                cols, below = slice(j * 256, j * 256 + 256), slice(j * 256, CAP)
                put(cols, h + 4, mm_tn(wts_ref[h, below, cols], dmix_ref[below, tile_at(h)]))
                put(cols, h + 12, mm_tn(ds_ref[below, cols], act_ref[below, tile_at(h + 8)]))

    def row_grads():
        @pl.loop(0, 4)
        def _(t):
            gated_ref[:, tile_at(t)] = mm_nt(pre_grad_ref[...], w_in_ref[tile_at(t), :]).astype(BF16)

        @pl.loop(0, CAP // ROWS)
        def _(r):
            rows = rows_at(r)
            hat, rstd = normalise(x_ref[rows, :].astype(F32))
            grad = norm_grad(gated_ref[rows, :].astype(F32), hat, rstd) + cot_ref[rows, :].astype(F32)
            grad = jnp.where(first_ref[rows, :] < CAP, grad, 0.0).astype(BF16)
            for e in range(8):
                row_grad_ref[e, pl.ds(8 * r, 8)] = grad[:, 128 * e : 128 * e + 128].reshape(8, 32, 128)

    embed()
    project()
    attend()
    mix()
    finish()
    back()
    for (low, high), out in zip(CUTS, (grad_y_out, grad_x_out, grad_z_out)):
        high = min(high, 4 * D)
        store(pre_grad_ref.at[:, low:high], out)
    row_grads()
    for copy in stores:
        copy.wait()


def lookup_kernel(items_ref, actions_ref, table_in, action_in, out_ref, table_ref, wide_ref, action_ref, rows_ref, sems):
    pieces = 8
    size = table_ref.shape[0] // pieces

    def load(n):
        rows = pl.ds(pl.multiple_of(n * size, size), size)
        return pltpu.make_async_copy(table_in.at[rows, :], table_ref.at[rows, :], sems.at[n])

    for n in range(pieces):
        load(n).start()
    action_ref[...] = action_in[...].astype(F32)

    @pl.loop(0, pieces)
    def _(n):
        load(n).wait()

        @pl.loop(0, size // 256)
        def _(k):
            rows = pl.ds(pl.multiple_of(n * size + k * 256, 256), 256)
            wide_ref[rows, :] = table_ref[rows, :].astype(F32)

    slots, owners = items_ref.shape

    @pl.loop(0, owners)
    def _(owner):
        for slot in range(slots):
            rows_ref[pl.ds(owner * slots + slot, 1), :] = (
                wide_ref[pl.ds(items_ref[slot, owner], 1), :]
                + action_ref[pl.ds(actions_ref[slot, owner], 1), :]
            )

    @pl.loop(0, owners // 8)
    def _(k):
        rows = pl.ds(pl.multiple_of(k * 8 * slots, 256), 8 * slots)
        out_ref[pl.ds(k * 8, 8)] = rows_ref[rows, :].astype(BF16).reshape(8, slots, 128)


def run_lookup(item_ids, action_ids, item_table, action_table):
    owners, slots = item_ids.shape
    return pl.pallas_call(
        lookup_kernel,
        out_shape=jax.ShapeDtypeStruct((owners, slots, 128), BF16),
        in_specs=[SMEM, SMEM, ANYWHERE, VMEM],
        out_specs=VMEM,
        scratch_shapes=[
            pltpu.VMEM(item_table.shape, BF16),
            pltpu.VMEM(item_table.shape, F32),
            pltpu.VMEM(action_table.shape, F32),
            pltpu.VMEM((owners * slots, 128), F32),
            pltpu.SemaphoreType.DMA((8,)),
        ],
        compiler_params=pltpu.CompilerParams(vmem_limit_bytes=58 << 20),
    )(item_ids.T, action_ids.T, item_table, action_table)


def run_layer(core, arrived, first, cotangent, gated_grad, w_in, w_out):
    part, whole = (CAP, D), (CAP, 4 * D)
    turned, square = (8, 128, CAP), (HEADS, CAP, CAP)
    scratch = [
        (w_out.shape, BF16), (part, BF16), (part, BF16), (part, BF16), (whole, BF16),
        (turned, BF16), (turned, BF16), (part, BF16), (whole, BF16), (whole, BF16), (square, BF16),
        (square, BF16), (part, F32), (part, BF16), (part, BF16), ((CAP, CAP), BF16),
        ((CAP, TILE), F32), ((CAP, TILE), F32),
    ]
    return pl.pallas_call(
        layer_kernel,
        out_shape=[
            jax.ShapeDtypeStruct(shape, BF16)
            for shape in [arrived.shape, part, turned, turned]
            + [(CAP, min(high, 4 * D) - low) for low, high in CUTS]
        ],
        in_specs=[SMEM, VMEM, VMEM, VMEM, VMEM, ANYWHERE, ANYWHERE],
        out_specs=[VMEM] + [ANYWHERE] * 6,
        scratch_shapes=[pltpu.VMEM(*one) for one in scratch]
        + [
            pltpu.SemaphoreType.DMA((2,)),
            pltpu.SemaphoreType.DMA((6,)),
        ],
        cost_estimate=pl.CostEstimate(
            flops=15_000_000_000, bytes_accessed=22 << 20, transcendentals=0
        ),
        compiler_params=pltpu.CompilerParams(vmem_limit_bytes=44 << 20),
    )(core, arrived, first, cotangent, w_in, gated_grad, w_out)


ANYWHERE = pl.BlockSpec(memory_space=pl.ANY)


def weight_grad_kernel(pairs, core_ref, *refs):
    operands, (send_ref, keep_ref, lhs_ref) = refs[:-3], refs[-3:]
    core, place = core_ref[0], 0
    for n in range(pairs):
        turned_ref, right_ref = operands[2 * n], operands[2 * n + 1]
        for y in range(4):
            lhs_ref[128 * y : 128 * y + 128] = turned_ref[2 * y + 1 - core]
            lhs_ref[512 + 128 * y : 640 + 128 * y] = turned_ref[2 * y + core]
        tiles = right_ref.shape[1] // TILE

        @pl.loop(0, tiles)
        def _(t, right_ref=right_ref, place=place):
            for low, out_ref in ((0, send_ref), (512, keep_ref)):
                out_ref[:, tile_at(t + place)] = mm(
                    lhs_ref[low : low + 512], right_ref[:, tile_at(t)]
                ).astype(BF16)

        place += tiles


def run_weight_grads(core, *operands):
    columns = sum(a.shape[1] for a in operands[1::2])
    return pl.pallas_call(
        functools.partial(weight_grad_kernel, len(operands) // 2),
        out_shape=[jax.ShapeDtypeStruct((512, columns), BF16)] * 2,
        in_specs=[SMEM] + [VMEM] * len(operands),
        out_specs=[VMEM] * 2,
        scratch_shapes=[pltpu.VMEM((D, CAP), BF16)],
        cost_estimate=pl.CostEstimate(
            flops=2 * CAP * D * columns, bytes_accessed=6 << 20, transcendentals=0
        ),
        compiler_params=pltpu.CompilerParams(vmem_limit_bytes=16 << 20),
    )(core, *operands)

VMEM = pl.BlockSpec(memory_space=pltpu.VMEM)
SMEM = pl.BlockSpec(memory_space=pltpu.SMEM)


def device_pairs(partner):
    pairs = []
    for device in range(128):
        emb, seq = divmod(device, 16)
        y, core, x, z = partner(emb // 2, emb % 2, seq // 4, seq % 4)
        pairs.append((device, (2 * y + core) * 16 + 4 * x + z))
    return pairs


CORE_PAIRS = device_pairs(lambda y, c, x, z: (y, 1 - c, x, z))
AXIS_PAIRS = {
    "y1": device_pairs(lambda y, c, x, z: (3 - y, c, x, z)),
    "x1": device_pairs(lambda y, c, x, z: (y, c, 3 - x, z)),
    "z1": device_pairs(lambda y, c, x, z: (y, c, x, 3 - z)),
}
BITS = ("y1", "y0", "x1", "x0", "z1", "z0")


ORDERS = (("y1", "x1", "z1"), ("x1", "z1", "y1"), ("z1", "y1", "x1"))


def cubes():
    found = {}
    for device in range(128):
        emb, seq = divmod(device, 16)
        y, core, x, z = emb // 2, emb % 2, seq // 4, seq % 4
        found.setdefault((y // 2, core, x // 2, z // 2), []).append((y % 2, x % 2, z % 2, device))
    return [[member[3] for member in sorted(cube)] for cube in found.values()]


def halve_kernel(bit_ref, kept_ref, arrived_ref, send_ref, keep_ref):
    bit, chunks = bit_ref[0], kept_ref.shape[2] // 16

    @pl.loop(0, kept_ref.shape[0])
    def _(outer):
        @pl.loop(0, chunks)
        def _(chunk):
            rows = pl.ds(pl.multiple_of(chunk * 16, 16), 16)
            for which, out_ref in ((1 - bit, send_ref), (bit, keep_ref)):
                out_ref[outer, rows, :] = (
                    kept_ref[outer, which, rows, :].astype(F32)
                    + arrived_ref[outer, which, rows, :].astype(F32)
                ).astype(BF16)


def halve(p, step, kept, arrived, bits):
    name = ORDERS[p][step]
    left = [b for b in BITS if b not in ORDERS[p][:step]]
    outer = 2 ** left.index(name)
    rows, columns = kept.shape
    shape = (outer, 2, rows // (2 * outer), columns)
    send, keep = pl.pallas_call(
        halve_kernel,
        out_shape=[jax.ShapeDtypeStruct((outer, shape[2], columns), BF16)] * 2,
        in_specs=[SMEM, VMEM, VMEM],
        out_specs=[VMEM, VMEM],
        cost_estimate=pl.CostEstimate(
            flops=rows * columns, bytes_accessed=6 * rows * columns, transcendentals=0
        ),
        compiler_params=pltpu.CompilerParams(vmem_limit_bytes=50 << 20),
    )(bits[name].astype(jnp.int32).reshape(1), kept.reshape(shape), arrived.reshape(shape))
    return send.reshape(rows // 2, columns), keep.reshape(rows // 2, columns)


def cross(p, step, send):
    return lax.ppermute(send, ("emb", "seq"), AXIS_PAIRS[ORDERS[p][step]])


def copy_kernel(in_ref, out_ref):
    out_ref[...] = in_ref[...]


def copy_out(values):
    return pl.pallas_call(
        copy_kernel,
        grid=(4,),
        out_shape=jax.ShapeDtypeStruct(values.shape, values.dtype),
        in_specs=[pl.BlockSpec((32, 32, 128), lambda k: (k, 0, 0))],
        out_specs=pl.BlockSpec((32, 32, 128), lambda k: (k, 0, 0)),
    )(values)


def swap(send):
    return lax.ppermute(send, ("emb", "seq"), CORE_PAIRS)


def gradient_shares(core, turned, pre_grads, gated_turned, cotangent, bits, row_grads):
    keeps, arrived = [None] * 3, [None] * 3
    pre_y, pre_x, pre_z = pre_grads
    send_y, keep_y = run_weight_grads(core, turned, pre_y)
    send_y, pre_x = lax.optimization_barrier((send_y, pre_x))
    got_y = swap(send_y)
    send_x, keep_x = run_weight_grads(core, turned, pre_x)
    got_x = swap(send_x)
    send_x, got_y = lax.optimization_barrier((send_x, got_y))
    send, keeps[0] = halve(0, 0, keep_y, got_y, bits)
    send, pre_z = lax.optimization_barrier((send, pre_z))
    arrived[0] = cross(0, 0, send)
    send_z, keep_z = run_weight_grads(core, turned, pre_z, gated_turned, cotangent)
    got_z = swap(send_z)
    send_z, got_x = lax.optimization_barrier((send_z, got_x))
    send, keeps[1] = halve(1, 0, keep_x, got_x, bits)
    arrived[1] = cross(1, 0, send)
    send, got_z, row_grads = lax.optimization_barrier((send, got_z, row_grads))
    send, keeps[2] = halve(2, 0, keep_z, got_z, bits)
    arrived[2] = cross(2, 0, send)
    row_grads = copy_out(row_grads)
    for step in (1, 2):
        for p in range(3):
            send, keeps[p] = halve(p, step, keeps[p], arrived[p], bits)
            arrived[p] = cross(p, step, send)
        if step == 1:
            *arrived, row_grads = lax.optimization_barrier((*arrived, row_grads))
    total = jnp.concatenate(
        [
            (keeps[p].astype(F32) + arrived[p].astype(F32)).astype(BF16).reshape(8, 8, -1)
            for p in range(3)
        ],
        axis=2,
    )
    total = lax.all_to_all(total, ("emb", "seq"), 0, 0, tiled=True, axis_index_groups=cubes())
    return jnp.sum(total.astype(F32), axis=0), row_grads


def shards(
    item_ids, action_ids, hist_len, hist_owner, item_table, action_table, w_in, w_out, cotangent
):
    emb_count = lax.axis_size("emb")
    seq_count = lax.axis_size("seq")
    device_count = emb_count * seq_count
    owner_count = item_ids.shape[0]
    slot_rows = item_ids.shape[1]
    column_width = item_table.shape[1]
    looked = run_lookup(item_ids, action_ids, item_table, action_table)
    arrived = lax.all_to_all(looked, ("emb", "seq"), split_axis=0, concat_axis=0, tiled=True)
    arrived = arrived.reshape(emb_count, seq_count, slot_rows, column_width)
    owner_index = lax.axis_index(("emb", "seq"))
    slot_start, occupied = slot_layout(hist_len, hist_owner, owner_index, CAP)
    first = jnp.where(occupied, slot_start, CAP).astype(jnp.int32)[:, None]
    emb, seq = lax.axis_index("emb"), lax.axis_index("seq")
    bits = {
        "y1": emb // 4, "y0": emb // 2 % 2,
        "x1": seq // 8, "x0": seq // 4 % 2, "z1": seq // 2 % 2, "z0": seq % 2,
    }
    core = (emb % 2).astype(jnp.int32).reshape(1)
    gated_grad = mm_nt(cotangent, w_out).astype(BF16)
    outgoing, result, turned, gated_turned, *pre_grads = run_layer(
        core, arrived, first, cotangent, gated_grad, w_in, w_out
    )
    outgoing = outgoing.reshape(owner_count, slot_rows, column_width)
    row_grads = lax.all_to_all(outgoing, ("emb", "seq"), split_axis=0, concat_axis=0, tiled=True)
    sums, row_grads = gradient_shares(
        core, turned, pre_grads, gated_turned, cotangent, bits, row_grads
    )
    in_share, out_share = sums[:, : 4 * D], sums[:, 4 * D :]
    return (result, row_grads, in_share / device_count, out_share / device_count)


def solution(mesh):
    in_specs = (
        P(None, "seq"),
        P(None, "seq"),
        P(),
        P(),
        P(None, "emb"),
        P(None, "emb"),
        P(),
        P(),
        P(("emb", "seq"), None),
    )
    out_specs = (
        P(("emb", "seq"), None),
        P(None, "seq", "emb"),
        P(("emb", "seq"), None),
        P(("emb", "seq"), None),
    )
    return jax.shard_map(shards, mesh=mesh, in_specs=in_specs, out_specs=out_specs, check_vma=False)
```

```python
import functools

import jax
import jax.numpy as jnp
from jax import lax
from jax.experimental import pallas as pl
from jax.experimental.pallas import tpu as pltpu
from jax.sharding import PartitionSpec as P

D = 1024
HEADS = 4
HEAD = 256
CAP = 512


EPSILON = 1e-06


def slot_layout(hist_len, hist_owner, owner_index, slot_count):
    chosen = hist_owner == owner_index
    lengths = jnp.where(chosen, hist_len, 0)
    hist_ends = jnp.cumsum(lengths, dtype=jnp.int32)
    starts = hist_ends - lengths
    slot_index = jnp.arange(slot_count, dtype=jnp.int32)
    inside = (
        chosen[None, :]
        & (starts[None, :] <= slot_index[:, None])
        & (slot_index[:, None] < hist_ends[None, :])
    )
    slot_start = jnp.sum(jnp.where(inside, starts[None, :], 0), axis=1, dtype=jnp.int32)
    occupied = jnp.any(inside, axis=1)
    return (slot_start, occupied)


F32, BF16 = jnp.float32, jnp.bfloat16
TILE = 256
CUTS = ((0, 1792), (1792, 3584), (3584, 5120))
ROWS = 256


def mm(a, b):
    return jnp.dot(a, b, preferred_element_type=F32)


def mm_nt(a, b):
    return lax.dot_general(a, b, (((1,), (1,)), ((), ())), preferred_element_type=F32)


def mm_tn(a, b):
    return lax.dot_general(a, b, (((0,), (0,)), ((), ())), preferred_element_type=F32)


def silu_pair(v):
    sig = 0.5 * jnp.tanh(0.5 * v) + 0.5
    act = v * sig
    return act, sig + act * (1.0 - sig)


def normalise(v):
    mean = jnp.mean(v, axis=-1, keepdims=True)
    centred = v - mean
    spread = jnp.mean(centred * centred, axis=-1, keepdims=True)
    rstd = lax.rsqrt(spread + EPSILON)
    return centred * rstd, rstd


def norm_grad(g, hat, rstd):
    return rstd * (
        g - jnp.mean(g, axis=-1, keepdims=True) - hat * jnp.mean(g * hat, axis=-1, keepdims=True)
    )


def tile_at(t):
    return pl.ds(pl.multiple_of(t * TILE, TILE), TILE)


def rows_at(r):
    return pl.ds(pl.multiple_of(r * ROWS, ROWS), ROWS)


def layer_kernel(
    core_ref, arrived_ref, first_ref, cot_ref, w_in_ref, gg_in, w_out_in,
    row_grad_ref, hist_out, turned_out, gated_turned_out, grad_y_out, grad_x_out, grad_z_out,
    w_out_ref, gg_ref, x_ref, hist_ref, pre_grad_ref, turned_ref, gated_turned_ref,
    normed_ref, act_ref, der_ref, wts_ref, wder_ref, mixed_ref, gated_ref, dmix_ref, ds_ref,
    pre_a_ref, pre_b_ref, in_sems, out_sems,
):
    core = core_ref[0]
    gg_load = pltpu.make_async_copy(gg_in, gg_ref, in_sems.at[0])
    w_out_load = pltpu.make_async_copy(w_out_in, w_out_ref, in_sems.at[1])
    gg_load.start()
    w_out_load.start()
    stores = []

    def store(src, dst):
        copy = pltpu.make_async_copy(src, dst, out_sems.at[len(stores)])
        copy.start()
        stores.append(copy)

    def turn(src, dst, k):
        for r in range(4):
            rows = slice(r * 128, r * 128 + 128)
            dst[k, :, rows] = src[rows, pl.ds(pl.multiple_of(128 * k, 128), 128)].T

    def embed():
        @pl.loop(0, CAP // ROWS)
        def _(r):
            rows = rows_at(r)
            x = jnp.concatenate(
                [arrived_ref[e, pl.ds(8 * r, 8)].reshape(ROWS, 128) for e in range(8)], axis=1
            ).astype(F32)
            x = jnp.where(first_ref[rows, :] < CAP, x, 0.0)
            x_ref[rows, :] = x.astype(BF16)
            normed_ref[rows, :] = normalise(x)[0].astype(BF16)

    def project():
        def multiply(into, t):
            into[...] = mm(normed_ref[...], w_in_ref[:, tile_at(t)])

        def activate(pre, t):
            act, der = silu_pair(pre[...])
            act_ref[:, tile_at(t)] = act.astype(BF16)
            der_ref[:, tile_at(t)] = der.astype(BF16)

        multiply(pre_a_ref, 0)

        @pl.loop(0, 7)
        def _(u):
            multiply(pre_b_ref, 2 * u + 1)
            activate(pre_a_ref, 2 * u)
            turn(normed_ref, turned_ref, u)
            multiply(pre_a_ref, 2 * u + 2)
            activate(pre_b_ref, 2 * u + 1)

        multiply(pre_b_ref, 15)
        activate(pre_a_ref, 14)
        turn(normed_ref, turned_ref, 7)
        activate(pre_b_ref, 15)

    def attend():
        @pl.loop(0, HEADS)
        def _(h):
            for i in range(2):
                rows, seen = slice(i * 256, i * 256 + 256), (i + 1) * 256
                v = act_ref[0:seen, tile_at(h + 4)]
                q = act_ref[rows, tile_at(h + 8)]
                k = act_ref[0:seen, tile_at(h + 12)]
                act, der = silu_pair(mm_nt(q, k) * HEAD**-0.5)
                at = lax.broadcasted_iota(jnp.int32, (256, seen), 0) + i * 256
                of = lax.broadcasted_iota(jnp.int32, (256, seen), 1)
                allowed = (of <= at) & (of >= first_ref[rows, :])
                wts = jnp.where(allowed, act * (1.0 / CAP), 0.0).astype(BF16)
                wts_ref[h, rows, 0:seen] = wts
                wder_ref[h, rows, 0:seen] = jnp.where(
                    allowed, der * (HEAD**-0.5 / CAP), 0.0
                ).astype(BF16)
                mixed_ref[rows, tile_at(h)] = mm(wts, v)

    def mix():
        gg_load.wait()

        @pl.loop(0, CAP // ROWS)
        def _(r):
            rows = rows_at(r)
            hat, rstd = normalise(mixed_ref[rows, :])
            gate = act_ref[rows, 0:D].astype(F32)
            gg = gg_ref[rows, :].astype(F32)
            gated_ref[rows, :] = (hat * gate).astype(BF16)
            pre_grad_ref[rows, 0:D] = (
                (gg * hat).astype(BF16).astype(F32) * der_ref[rows, 0:D].astype(F32)
            ).astype(BF16)
            dmix_ref[rows, :] = norm_grad(gg * gate, hat, rstd).astype(BF16)

    def finish():
        w_out_load.wait()

        @pl.loop(0, 4)
        def _(t):
            hist_ref[:, tile_at(t)] = (
                x_ref[:, tile_at(t)].astype(F32) + mm(gated_ref[...], w_out_ref[:, tile_at(t)])
            ).astype(BF16)
            turn(gated_ref, gated_turned_ref, 2 * t)
            turn(gated_ref, gated_turned_ref, 2 * t + 1)

        store(hist_ref, hist_out)
        store(turned_ref, turned_out)
        store(gated_turned_ref, gated_turned_out)

    def put(rows, t, grad):
        pre_grad_ref[rows, tile_at(t)] = (
            grad.astype(BF16).astype(F32) * der_ref[rows, tile_at(t)].astype(F32)
        ).astype(BF16)

    def back():
        @pl.loop(0, HEADS)
        def _(h):
            for i in range(2):
                rows, seen = slice(i * 256, i * 256 + 256), (i + 1) * 256
                dmix = dmix_ref[rows, tile_at(h)]
                dw = mm_nt(dmix, act_ref[0:seen, tile_at(h + 4)]).astype(BF16).astype(F32)
                ds = (dw * wder_ref[h, rows, 0:seen].astype(F32)).astype(BF16)
                ds_ref[rows, 0:seen] = ds
                put(rows, h + 8, mm(ds, act_ref[0:seen, tile_at(h + 12)]))
            for j in range(2):
                cols, below = slice(j * 256, j * 256 + 256), slice(j * 256, CAP)
                put(cols, h + 4, mm_tn(wts_ref[h, below, cols], dmix_ref[below, tile_at(h)]))
                put(cols, h + 12, mm_tn(ds_ref[below, cols], act_ref[below, tile_at(h + 8)]))

    def row_grads():
        @pl.loop(0, 4)
        def _(t):
            gated_ref[:, tile_at(t)] = mm_nt(pre_grad_ref[...], w_in_ref[tile_at(t), :]).astype(BF16)

        @pl.loop(0, CAP // ROWS)
        def _(r):
            rows = rows_at(r)
            hat, rstd = normalise(x_ref[rows, :].astype(F32))
            grad = norm_grad(gated_ref[rows, :].astype(F32), hat, rstd) + cot_ref[rows, :].astype(F32)
            grad = jnp.where(first_ref[rows, :] < CAP, grad, 0.0).astype(BF16)
            for e in range(8):
                row_grad_ref[e, pl.ds(8 * r, 8)] = grad[:, 128 * e : 128 * e + 128].reshape(8, 32, 128)

    embed()
    project()
    attend()
    mix()
    finish()
    back()
    for (low, high), out in zip(CUTS, (grad_y_out, grad_x_out, grad_z_out)):
        high = min(high, 4 * D)
        store(pre_grad_ref.at[:, low:high], out)
    row_grads()
    for copy in stores:
        copy.wait()


def lookup_kernel(items_ref, actions_ref, table_in, action_in, out_ref, table_ref, wide_ref, action_ref, rows_ref, sems):
    pieces = 8
    size = table_ref.shape[0] // pieces

    def load(n):
        rows = pl.ds(pl.multiple_of(n * size, size), size)
        return pltpu.make_async_copy(table_in.at[rows, :], table_ref.at[rows, :], sems.at[n])

    for n in range(pieces):
        load(n).start()
    action_ref[...] = action_in[...].astype(F32)

    @pl.loop(0, pieces)
    def _(n):
        load(n).wait()

        @pl.loop(0, size // 1024)
        def _(k):
            rows = pl.ds(pl.multiple_of(n * size + k * 1024, 1024), 1024)
            wide_ref[rows, :] = table_ref[rows, :].astype(F32)

    slots, owners = items_ref.shape

    @pl.loop(0, owners // 4)
    def _(group):
        for n in range(4 * slots):
            owner, slot = 4 * group + n // slots, n % slots
            rows_ref[pl.ds(4 * slots * group + n, 1), :] = (
                wide_ref[pl.ds(items_ref[slot, owner], 1), :]
                + action_ref[pl.ds(actions_ref[slot, owner], 1), :]
            )

    @pl.loop(0, owners // 32)
    def _(k):
        rows = pl.ds(pl.multiple_of(k * 32 * slots, 1024), 32 * slots)
        out_ref[pl.ds(k * 32, 32)] = rows_ref[rows, :].astype(BF16).reshape(32, slots, 128)


def run_lookup(item_ids, action_ids, item_table, action_table):
    owners, slots = item_ids.shape
    return pl.pallas_call(
        lookup_kernel,
        out_shape=jax.ShapeDtypeStruct((owners, slots, 128), BF16),
        in_specs=[SMEM, SMEM, ANYWHERE, VMEM],
        out_specs=VMEM,
        scratch_shapes=[
            pltpu.VMEM(item_table.shape, BF16),
            pltpu.VMEM(item_table.shape, F32),
            pltpu.VMEM(action_table.shape, F32),
            pltpu.VMEM((owners * slots, 128), F32),
            pltpu.SemaphoreType.DMA((8,)),
        ],
        compiler_params=pltpu.CompilerParams(vmem_limit_bytes=58 << 20),
    )(item_ids.T, action_ids.T, item_table, action_table)


def run_layer(core, arrived, first, cotangent, gated_grad, w_in, w_out):
    part, whole = (CAP, D), (CAP, 4 * D)
    turned, square = (8, 128, CAP), (HEADS, CAP, CAP)
    scratch = [
        (w_out.shape, BF16), (part, BF16), (part, BF16), (part, BF16), (whole, BF16),
        (turned, BF16), (turned, BF16), (part, BF16), (whole, BF16), (whole, BF16), (square, BF16),
        (square, BF16), (part, F32), (part, BF16), (part, BF16), ((CAP, CAP), BF16),
        ((CAP, TILE), F32), ((CAP, TILE), F32),
    ]
    return pl.pallas_call(
        layer_kernel,
        out_shape=[
            jax.ShapeDtypeStruct(shape, BF16)
            for shape in [arrived.shape, part, turned, turned]
            + [(CAP, min(high, 4 * D) - low) for low, high in CUTS]
        ],
        in_specs=[SMEM, VMEM, VMEM, VMEM, VMEM, ANYWHERE, ANYWHERE],
        out_specs=[VMEM] + [ANYWHERE] * 6,
        scratch_shapes=[pltpu.VMEM(*one) for one in scratch]
        + [
            pltpu.SemaphoreType.DMA((2,)),
            pltpu.SemaphoreType.DMA((6,)),
        ],
        cost_estimate=pl.CostEstimate(
            flops=15_000_000_000, bytes_accessed=22 << 20, transcendentals=0
        ),
        compiler_params=pltpu.CompilerParams(vmem_limit_bytes=44 << 20),
    )(core, arrived, first, cotangent, w_in, gated_grad, w_out)


ANYWHERE = pl.BlockSpec(memory_space=pl.ANY)


def weight_grad_kernel(pairs, core_ref, *refs):
    operands, (send_ref, keep_ref, lhs_ref) = refs[:-3], refs[-3:]
    core, place = core_ref[0], 0
    for n in range(pairs):
        turned_ref, right_ref = operands[2 * n], operands[2 * n + 1]
        for y in range(4):
            lhs_ref[128 * y : 128 * y + 128] = turned_ref[2 * y + 1 - core]
            lhs_ref[512 + 128 * y : 640 + 128 * y] = turned_ref[2 * y + core]
        tiles = right_ref.shape[1] // TILE

        @pl.loop(0, tiles)
        def _(t, right_ref=right_ref, place=place):
            for low, out_ref in ((0, send_ref), (512, keep_ref)):
                out_ref[:, tile_at(t + place)] = mm(
                    lhs_ref[low : low + 512], right_ref[:, tile_at(t)]
                ).astype(BF16)

        place += tiles


def run_weight_grads(core, *operands):
    columns = sum(a.shape[1] for a in operands[1::2])
    return pl.pallas_call(
        functools.partial(weight_grad_kernel, len(operands) // 2),
        out_shape=[jax.ShapeDtypeStruct((512, columns), BF16)] * 2,
        in_specs=[SMEM] + [VMEM] * len(operands),
        out_specs=[VMEM] * 2,
        scratch_shapes=[pltpu.VMEM((D, CAP), BF16)],
        cost_estimate=pl.CostEstimate(
            flops=2 * CAP * D * columns, bytes_accessed=6 << 20, transcendentals=0
        ),
        compiler_params=pltpu.CompilerParams(vmem_limit_bytes=16 << 20),
    )(core, *operands)

VMEM = pl.BlockSpec(memory_space=pltpu.VMEM)
SMEM = pl.BlockSpec(memory_space=pltpu.SMEM)


def device_pairs(partner):
    pairs = []
    for device in range(128):
        emb, seq = divmod(device, 16)
        y, core, x, z = partner(emb // 2, emb % 2, seq // 4, seq % 4)
        pairs.append((device, (2 * y + core) * 16 + 4 * x + z))
    return pairs


CORE_PAIRS = device_pairs(lambda y, c, x, z: (y, 1 - c, x, z))
AXIS_PAIRS = {
    "y1": device_pairs(lambda y, c, x, z: (3 - y, c, x, z)),
    "x1": device_pairs(lambda y, c, x, z: (y, c, 3 - x, z)),
    "z1": device_pairs(lambda y, c, x, z: (y, c, x, 3 - z)),
}
BITS = ("y1", "y0", "x1", "x0", "z1", "z0")


ORDERS = (("y1", "x1", "z1"), ("x1", "z1", "y1"), ("z1", "y1", "x1"))


def cubes():
    found = {}
    for device in range(128):
        emb, seq = divmod(device, 16)
        y, core, x, z = emb // 2, emb % 2, seq // 4, seq % 4
        found.setdefault((y // 2, core, x // 2, z // 2), []).append((y % 2, x % 2, z % 2, device))
    return [[member[3] for member in sorted(cube)] for cube in found.values()]


def halve_kernel(bit_ref, kept_ref, arrived_ref, send_ref, keep_ref):
    bit, chunks = bit_ref[0], kept_ref.shape[2] // 16

    @pl.loop(0, kept_ref.shape[0])
    def _(outer):
        @pl.loop(0, chunks)
        def _(chunk):
            rows = pl.ds(pl.multiple_of(chunk * 16, 16), 16)
            for which, out_ref in ((1 - bit, send_ref), (bit, keep_ref)):
                out_ref[outer, rows, :] = (
                    kept_ref[outer, which, rows, :].astype(F32)
                    + arrived_ref[outer, which, rows, :].astype(F32)
                ).astype(BF16)


def halve(p, step, kept, arrived, bits):
    name = ORDERS[p][step]
    left = [b for b in BITS if b not in ORDERS[p][:step]]
    outer = 2 ** left.index(name)
    rows, columns = kept.shape
    shape = (outer, 2, rows // (2 * outer), columns)
    send, keep = pl.pallas_call(
        halve_kernel,
        out_shape=[jax.ShapeDtypeStruct((outer, shape[2], columns), BF16)] * 2,
        in_specs=[SMEM, VMEM, VMEM],
        out_specs=[VMEM, VMEM],
        cost_estimate=pl.CostEstimate(
            flops=rows * columns, bytes_accessed=6 * rows * columns, transcendentals=0
        ),
        compiler_params=pltpu.CompilerParams(vmem_limit_bytes=50 << 20),
    )(bits[name].astype(jnp.int32).reshape(1), kept.reshape(shape), arrived.reshape(shape))
    return send.reshape(rows // 2, columns), keep.reshape(rows // 2, columns)


def cross(p, step, send):
    return lax.ppermute(send, ("emb", "seq"), AXIS_PAIRS[ORDERS[p][step]])


def copy_kernel(in_ref, out_ref):
    out_ref[...] = in_ref[...]


def copy_out(values):
    return pl.pallas_call(
        copy_kernel,
        grid=(4,),
        out_shape=jax.ShapeDtypeStruct(values.shape, values.dtype),
        in_specs=[pl.BlockSpec((32, 32, 128), lambda k: (k, 0, 0))],
        out_specs=pl.BlockSpec((32, 32, 128), lambda k: (k, 0, 0)),
    )(values)


def swap(send):
    return lax.ppermute(send, ("emb", "seq"), CORE_PAIRS)


def gradient_shares(core, turned, pre_grads, gated_turned, cotangent, bits, row_grads):
    keeps, arrived = [None] * 3, [None] * 3
    pre_y, pre_x, pre_z = pre_grads
    send_y, keep_y = run_weight_grads(core, turned, pre_y)
    send_y, pre_x = lax.optimization_barrier((send_y, pre_x))
    got_y = swap(send_y)
    send_x, keep_x = run_weight_grads(core, turned, pre_x)
    got_x = swap(send_x)
    send_x, got_y = lax.optimization_barrier((send_x, got_y))
    send, keeps[0] = halve(0, 0, keep_y, got_y, bits)
    send, pre_z = lax.optimization_barrier((send, pre_z))
    arrived[0] = cross(0, 0, send)
    send_z, keep_z = run_weight_grads(core, turned, pre_z, gated_turned, cotangent)
    got_z = swap(send_z)
    send_z, got_x = lax.optimization_barrier((send_z, got_x))
    send, keeps[1] = halve(1, 0, keep_x, got_x, bits)
    arrived[1] = cross(1, 0, send)
    send, got_z, row_grads = lax.optimization_barrier((send, got_z, row_grads))
    send, keeps[2] = halve(2, 0, keep_z, got_z, bits)
    arrived[2] = cross(2, 0, send)
    row_grads = copy_out(row_grads)
    for step in (1, 2):
        for p in range(3):
            send, keeps[p] = halve(p, step, keeps[p], arrived[p], bits)
            arrived[p] = cross(p, step, send)
        if step == 1:
            *arrived, row_grads = lax.optimization_barrier((*arrived, row_grads))
    total = jnp.concatenate(
        [
            (keeps[p].astype(F32) + arrived[p].astype(F32)).astype(BF16).reshape(8, 8, -1)
            for p in range(3)
        ],
        axis=2,
    )
    total = lax.all_to_all(total, ("emb", "seq"), 0, 0, tiled=True, axis_index_groups=cubes())
    return jnp.sum(total.astype(F32), axis=0), row_grads


def shards(
    item_ids, action_ids, hist_len, hist_owner, item_table, action_table, w_in, w_out, cotangent
):
    emb_count = lax.axis_size("emb")
    seq_count = lax.axis_size("seq")
    device_count = emb_count * seq_count
    owner_count = item_ids.shape[0]
    slot_rows = item_ids.shape[1]
    column_width = item_table.shape[1]
    looked = run_lookup(item_ids, action_ids, item_table, action_table)
    arrived = lax.all_to_all(looked, ("emb", "seq"), split_axis=0, concat_axis=0, tiled=True)
    arrived = arrived.reshape(emb_count, seq_count, slot_rows, column_width)
    owner_index = lax.axis_index(("emb", "seq"))
    slot_start, occupied = slot_layout(hist_len, hist_owner, owner_index, CAP)
    first = jnp.where(occupied, slot_start, CAP).astype(jnp.int32)[:, None]
    emb, seq = lax.axis_index("emb"), lax.axis_index("seq")
    bits = {
        "y1": emb // 4, "y0": emb // 2 % 2,
        "x1": seq // 8, "x0": seq // 4 % 2, "z1": seq // 2 % 2, "z0": seq % 2,
    }
    core = (emb % 2).astype(jnp.int32).reshape(1)
    gated_grad = mm_nt(cotangent, w_out).astype(BF16)
    outgoing, result, turned, gated_turned, *pre_grads = run_layer(
        core, arrived, first, cotangent, gated_grad, w_in, w_out
    )
    outgoing = outgoing.reshape(owner_count, slot_rows, column_width)
    row_grads = lax.all_to_all(outgoing, ("emb", "seq"), split_axis=0, concat_axis=0, tiled=True)
    sums, row_grads = gradient_shares(
        core, turned, pre_grads, gated_turned, cotangent, bits, row_grads
    )
    in_share, out_share = sums[:, : 4 * D], sums[:, 4 * D :]
    return (result, row_grads, in_share / device_count, out_share / device_count)


def solution(mesh):
    in_specs = (
        P(None, "seq"),
        P(None, "seq"),
        P(),
        P(),
        P(None, "emb"),
        P(None, "emb"),
        P(),
        P(),
        P(("emb", "seq"), None),
    )
    out_specs = (
        P(("emb", "seq"), None),
        P(None, "seq", "emb"),
        P(("emb", "seq"), None),
        P(("emb", "seq"), None),
    )
    return jax.shard_map(shards, mesh=mesh, in_specs=in_specs, out_specs=out_specs, check_vma=False)
```

```python
import functools

import jax
import jax.numpy as jnp
from jax import lax
from jax.experimental import pallas as pl
from jax.experimental.pallas import tpu as pltpu
from jax.sharding import PartitionSpec as P

D = 1024
HEADS = 4
HEAD = 256
CAP = 512


EPSILON = 1e-06


def slot_layout(hist_len, hist_owner, owner_index, slot_count):
    chosen = hist_owner == owner_index
    lengths = jnp.where(chosen, hist_len, 0)
    hist_ends = jnp.cumsum(lengths, dtype=jnp.int32)
    starts = hist_ends - lengths
    slot_index = jnp.arange(slot_count, dtype=jnp.int32)
    inside = (
        chosen[None, :]
        & (starts[None, :] <= slot_index[:, None])
        & (slot_index[:, None] < hist_ends[None, :])
    )
    slot_start = jnp.sum(jnp.where(inside, starts[None, :], 0), axis=1, dtype=jnp.int32)
    occupied = jnp.any(inside, axis=1)
    return (slot_start, occupied)


F32, BF16 = jnp.float32, jnp.bfloat16
TILE = 256
CUTS = ((0, 1792), (1792, 3584), (3584, 5120))
ROWS = 256


def mm(a, b):
    return jnp.dot(a, b, preferred_element_type=F32)


def mm_nt(a, b):
    return lax.dot_general(a, b, (((1,), (1,)), ((), ())), preferred_element_type=F32)


def mm_tn(a, b):
    return lax.dot_general(a, b, (((0,), (0,)), ((), ())), preferred_element_type=F32)


def silu_pair(v):
    sig = 0.5 * jnp.tanh(0.5 * v) + 0.5
    act = v * sig
    return act, sig + act * (1.0 - sig)


def normalise(v):
    mean = jnp.mean(v, axis=-1, keepdims=True)
    centred = v - mean
    spread = jnp.mean(centred * centred, axis=-1, keepdims=True)
    rstd = lax.rsqrt(spread + EPSILON)
    return centred * rstd, rstd


def norm_grad(g, hat, rstd):
    return rstd * (
        g - jnp.mean(g, axis=-1, keepdims=True) - hat * jnp.mean(g * hat, axis=-1, keepdims=True)
    )


def tile_at(t):
    return pl.ds(pl.multiple_of(t * TILE, TILE), TILE)


def rows_at(r):
    return pl.ds(pl.multiple_of(r * ROWS, ROWS), ROWS)


def layer_kernel(
    core_ref, arrived_ref, first_ref, cot_ref, w_in_ref, gg_in, w_out_in,
    row_grad_ref, hist_out, turned_out, gated_turned_out, grad_y_out, grad_x_out, grad_z_out,
    w_out_ref, gg_ref, x_ref, hist_ref, pre_grad_ref, turned_ref, gated_turned_ref,
    normed_ref, act_ref, der_ref, wts_ref, wder_ref, mixed_ref, gated_ref, dmix_ref, ds_ref,
    pre_a_ref, pre_b_ref, in_sems, out_sems,
):
    core = core_ref[0]
    gg_load = pltpu.make_async_copy(gg_in, gg_ref, in_sems.at[0])
    w_out_load = pltpu.make_async_copy(w_out_in, w_out_ref, in_sems.at[1])
    gg_load.start()
    w_out_load.start()
    stores = []

    def store(src, dst):
        copy = pltpu.make_async_copy(src, dst, out_sems.at[len(stores)])
        copy.start()
        stores.append(copy)

    def turn(src, dst, k):
        for r in range(4):
            rows = slice(r * 128, r * 128 + 128)
            dst[k, :, rows] = src[rows, pl.ds(pl.multiple_of(128 * k, 128), 128)].T

    def embed():
        @pl.loop(0, CAP // ROWS)
        def _(r):
            rows = rows_at(r)
            x = jnp.concatenate(
                [arrived_ref[e, pl.ds(8 * r, 8)].reshape(ROWS, 128) for e in range(8)], axis=1
            ).astype(F32)
            x = jnp.where(first_ref[rows, :] < CAP, x, 0.0)
            x_ref[rows, :] = x.astype(BF16)
            normed_ref[rows, :] = normalise(x)[0].astype(BF16)

    def project():
        def multiply(into, t):
            into[...] = mm(normed_ref[...], w_in_ref[:, tile_at(t)])

        def activate(pre, t):
            act, der = silu_pair(pre[...])
            act_ref[:, tile_at(t)] = act.astype(BF16)
            der_ref[:, tile_at(t)] = der.astype(BF16)

        multiply(pre_a_ref, 0)

        @pl.loop(0, 7)
        def _(u):
            multiply(pre_b_ref, 2 * u + 1)
            activate(pre_a_ref, 2 * u)
            turn(normed_ref, turned_ref, u)
            multiply(pre_a_ref, 2 * u + 2)
            activate(pre_b_ref, 2 * u + 1)

        multiply(pre_b_ref, 15)
        activate(pre_a_ref, 14)
        turn(normed_ref, turned_ref, 7)
        activate(pre_b_ref, 15)

    def attend():
        @pl.loop(0, HEADS)
        def _(h):
            for i in range(2):
                rows, seen = slice(i * 256, i * 256 + 256), (i + 1) * 256
                v = act_ref[0:seen, tile_at(h + 4)]
                q = act_ref[rows, tile_at(h + 8)]
                k = act_ref[0:seen, tile_at(h + 12)]
                act, der = silu_pair(mm_nt(q, k) * HEAD**-0.5)
                at = lax.broadcasted_iota(jnp.int32, (256, seen), 0) + i * 256
                of = lax.broadcasted_iota(jnp.int32, (256, seen), 1)
                allowed = (of <= at) & (of >= first_ref[rows, :])
                wts = jnp.where(allowed, act * (1.0 / CAP), 0.0).astype(BF16)
                wts_ref[h, rows, 0:seen] = wts
                wder_ref[h, rows, 0:seen] = jnp.where(
                    allowed, der * (HEAD**-0.5 / CAP), 0.0
                ).astype(BF16)
                mixed_ref[rows, tile_at(h)] = mm(wts, v)

    def mix():
        gg_load.wait()

        @pl.loop(0, CAP // ROWS)
        def _(r):
            rows = rows_at(r)
            hat, rstd = normalise(mixed_ref[rows, :])
            gate = act_ref[rows, 0:D].astype(F32)
            gg = gg_ref[rows, :].astype(F32)
            gated_ref[rows, :] = (hat * gate).astype(BF16)
            pre_grad_ref[rows, 0:D] = (
                (gg * hat).astype(BF16).astype(F32) * der_ref[rows, 0:D].astype(F32)
            ).astype(BF16)
            dmix_ref[rows, :] = norm_grad(gg * gate, hat, rstd).astype(BF16)

    def finish():
        w_out_load.wait()

        @pl.loop(0, 4)
        def _(t):
            hist_ref[:, tile_at(t)] = (
                x_ref[:, tile_at(t)].astype(F32) + mm(gated_ref[...], w_out_ref[:, tile_at(t)])
            ).astype(BF16)
            turn(gated_ref, gated_turned_ref, 2 * t)
            turn(gated_ref, gated_turned_ref, 2 * t + 1)

        store(hist_ref, hist_out)
        store(turned_ref, turned_out)
        store(gated_turned_ref, gated_turned_out)

    def put(rows, t, grad):
        pre_grad_ref[rows, tile_at(t)] = (
            grad.astype(BF16).astype(F32) * der_ref[rows, tile_at(t)].astype(F32)
        ).astype(BF16)

    def back():
        @pl.loop(0, HEADS)
        def _(h):
            for i in range(2):
                rows, seen = slice(i * 256, i * 256 + 256), (i + 1) * 256
                dmix = dmix_ref[rows, tile_at(h)]
                dw = mm_nt(dmix, act_ref[0:seen, tile_at(h + 4)]).astype(BF16).astype(F32)
                ds = (dw * wder_ref[h, rows, 0:seen].astype(F32)).astype(BF16)
                ds_ref[rows, 0:seen] = ds
                put(rows, h + 8, mm(ds, act_ref[0:seen, tile_at(h + 12)]))
            for j in range(2):
                cols, below = slice(j * 256, j * 256 + 256), slice(j * 256, CAP)
                put(cols, h + 4, mm_tn(wts_ref[h, below, cols], dmix_ref[below, tile_at(h)]))
                put(cols, h + 12, mm_tn(ds_ref[below, cols], act_ref[below, tile_at(h + 8)]))

    def row_grads():
        @pl.loop(0, 4)
        def _(t):
            gated_ref[:, tile_at(t)] = mm_nt(pre_grad_ref[...], w_in_ref[tile_at(t), :]).astype(BF16)

        @pl.loop(0, CAP // ROWS)
        def _(r):
            rows = rows_at(r)
            hat, rstd = normalise(x_ref[rows, :].astype(F32))
            grad = norm_grad(gated_ref[rows, :].astype(F32), hat, rstd) + cot_ref[rows, :].astype(F32)
            grad = jnp.where(first_ref[rows, :] < CAP, grad, 0.0).astype(BF16)
            for e in range(8):
                row_grad_ref[e, pl.ds(8 * r, 8)] = grad[:, 128 * e : 128 * e + 128].reshape(8, 32, 128)

    embed()
    project()
    attend()
    mix()
    finish()
    back()
    for (low, high), out in zip(CUTS, (grad_y_out, grad_x_out, grad_z_out)):
        high = min(high, 4 * D)
        store(pre_grad_ref.at[:, low:high], out)
    row_grads()
    for copy in stores:
        copy.wait()


def lookup_kernel(items_ref, actions_ref, table_in, action_in, out_ref, table_ref, wide_ref, action_ref, rows_ref, sems):
    pieces = 8
    size = table_ref.shape[0] // pieces

    def load(n):
        rows = pl.ds(pl.multiple_of(n * size, size), size)
        return pltpu.make_async_copy(table_in.at[rows, :], table_ref.at[rows, :], sems.at[n])

    for n in range(pieces):
        load(n).start()
    action_ref[...] = action_in[...].astype(F32)

    @pl.loop(0, pieces)
    def _(n):
        load(n).wait()

        @pl.loop(0, size // 1024)
        def _(k):
            rows = pl.ds(pl.multiple_of(n * size + k * 1024, 1024), 1024)
            wide_ref[rows, :] = table_ref[rows, :].astype(F32)

    slots, owners = items_ref.shape

    @pl.loop(0, owners // 4)
    def _(group):
        for n in range(4 * slots):
            owner, slot = 4 * group + n // slots, n % slots
            rows_ref[pl.ds(4 * slots * group + n, 1), :] = (
                wide_ref[pl.ds(items_ref[slot, owner], 1), :]
                + action_ref[pl.ds(actions_ref[slot, owner], 1), :]
            )

    @pl.loop(0, owners // 32)
    def _(k):
        rows = pl.ds(pl.multiple_of(k * 32 * slots, 1024), 32 * slots)
        out_ref[pl.ds(k * 32, 32)] = rows_ref[rows, :].astype(BF16).reshape(32, slots, 128)


def run_lookup(item_ids, action_ids, item_table, action_table):
    owners, slots = item_ids.shape
    return pl.pallas_call(
        lookup_kernel,
        out_shape=jax.ShapeDtypeStruct((owners, slots, 128), BF16),
        in_specs=[SMEM, SMEM, ANYWHERE, VMEM],
        out_specs=VMEM,
        scratch_shapes=[
            pltpu.VMEM(item_table.shape, BF16),
            pltpu.VMEM(item_table.shape, F32),
            pltpu.VMEM(action_table.shape, F32),
            pltpu.VMEM((owners * slots, 128), F32),
            pltpu.SemaphoreType.DMA((8,)),
        ],
        compiler_params=pltpu.CompilerParams(vmem_limit_bytes=58 << 20),
    )(item_ids.T, action_ids.T, item_table, action_table)


def run_layer(core, arrived, first, cotangent, gated_grad, w_in, w_out):
    part, whole = (CAP, D), (CAP, 4 * D)
    turned, square = (8, 128, CAP), (HEADS, CAP, CAP)
    scratch = [
        (w_out.shape, BF16), (part, BF16), (part, BF16), (part, BF16), (whole, BF16),
        (turned, BF16), (turned, BF16), (part, BF16), (whole, BF16), (whole, BF16), (square, BF16),
        (square, BF16), (part, F32), (part, BF16), (part, BF16), ((CAP, CAP), BF16),
        ((CAP, TILE), F32), ((CAP, TILE), F32),
    ]
    return pl.pallas_call(
        layer_kernel,
        out_shape=[
            jax.ShapeDtypeStruct(shape, BF16)
            for shape in [arrived.shape, part, turned, turned]
            + [(CAP, min(high, 4 * D) - low) for low, high in CUTS]
        ],
        in_specs=[SMEM, VMEM, VMEM, VMEM, VMEM, ANYWHERE, ANYWHERE],
        out_specs=[VMEM] + [ANYWHERE] * 6,
        scratch_shapes=[pltpu.VMEM(*one) for one in scratch]
        + [
            pltpu.SemaphoreType.DMA((2,)),
            pltpu.SemaphoreType.DMA((6,)),
        ],
        cost_estimate=pl.CostEstimate(
            flops=15_000_000_000, bytes_accessed=22 << 20, transcendentals=0
        ),
        compiler_params=pltpu.CompilerParams(vmem_limit_bytes=44 << 20),
    )(core, arrived, first, cotangent, w_in, gated_grad, w_out)


ANYWHERE = pl.BlockSpec(memory_space=pl.ANY)


def weight_grad_kernel(pairs, core_ref, *refs):
    operands, (send_ref, keep_ref, lhs_ref) = refs[:-3], refs[-3:]
    core, place = core_ref[0], 0
    for n in range(pairs):
        turned_ref, right_ref = operands[2 * n], operands[2 * n + 1]
        for y in range(4):
            lhs_ref[128 * y : 128 * y + 128] = turned_ref[2 * y + 1 - core]
            lhs_ref[512 + 128 * y : 640 + 128 * y] = turned_ref[2 * y + core]
        tiles = right_ref.shape[1] // TILE

        @pl.loop(0, tiles)
        def _(t, right_ref=right_ref, place=place):
            sums = mm(lhs_ref[...], right_ref[:, tile_at(t)]).astype(BF16)
            send_ref[:, tile_at(t + place)] = sums[0:512]
            keep_ref[:, tile_at(t + place)] = sums[512:1024]

        place += tiles


def run_weight_grads(core, *operands):
    columns = sum(a.shape[1] for a in operands[1::2])
    return pl.pallas_call(
        functools.partial(weight_grad_kernel, len(operands) // 2),
        out_shape=[jax.ShapeDtypeStruct((512, columns), BF16)] * 2,
        in_specs=[SMEM] + [VMEM] * len(operands),
        out_specs=[VMEM] * 2,
        scratch_shapes=[pltpu.VMEM((D, CAP), BF16)],
        cost_estimate=pl.CostEstimate(
            flops=2 * CAP * D * columns, bytes_accessed=6 << 20, transcendentals=0
        ),
        compiler_params=pltpu.CompilerParams(vmem_limit_bytes=16 << 20),
    )(core, *operands)

VMEM = pl.BlockSpec(memory_space=pltpu.VMEM)
SMEM = pl.BlockSpec(memory_space=pltpu.SMEM)


def device_pairs(partner):
    pairs = []
    for device in range(128):
        emb, seq = divmod(device, 16)
        y, core, x, z = partner(emb // 2, emb % 2, seq // 4, seq % 4)
        pairs.append((device, (2 * y + core) * 16 + 4 * x + z))
    return pairs


CORE_PAIRS = device_pairs(lambda y, c, x, z: (y, 1 - c, x, z))
AXIS_PAIRS = {
    "y1": device_pairs(lambda y, c, x, z: (3 - y, c, x, z)),
    "x1": device_pairs(lambda y, c, x, z: (y, c, 3 - x, z)),
    "z1": device_pairs(lambda y, c, x, z: (y, c, x, 3 - z)),
}
BITS = ("y1", "y0", "x1", "x0", "z1", "z0")


ORDERS = (("y1", "x1", "z1"), ("x1", "z1", "y1"), ("z1", "y1", "x1"))


def cubes():
    found = {}
    for device in range(128):
        emb, seq = divmod(device, 16)
        y, core, x, z = emb // 2, emb % 2, seq // 4, seq % 4
        found.setdefault((y // 2, core, x // 2, z // 2), []).append((y % 2, x % 2, z % 2, device))
    return [[member[3] for member in sorted(cube)] for cube in found.values()]


def halve_kernel(bit_ref, kept_ref, arrived_ref, send_ref, keep_ref):
    bit, chunks = bit_ref[0], kept_ref.shape[2] // 16

    @pl.loop(0, kept_ref.shape[0])
    def _(outer):
        @pl.loop(0, chunks)
        def _(chunk):
            rows = pl.ds(pl.multiple_of(chunk * 16, 16), 16)
            for which, out_ref in ((1 - bit, send_ref), (bit, keep_ref)):
                out_ref[outer, rows, :] = (
                    kept_ref[outer, which, rows, :].astype(F32)
                    + arrived_ref[outer, which, rows, :].astype(F32)
                ).astype(BF16)


def halve(p, step, kept, arrived, bits):
    name = ORDERS[p][step]
    left = [b for b in BITS if b not in ORDERS[p][:step]]
    outer = 2 ** left.index(name)
    rows, columns = kept.shape
    shape = (outer, 2, rows // (2 * outer), columns)
    send, keep = pl.pallas_call(
        halve_kernel,
        out_shape=[jax.ShapeDtypeStruct((outer, shape[2], columns), BF16)] * 2,
        in_specs=[SMEM, VMEM, VMEM],
        out_specs=[VMEM, VMEM],
        cost_estimate=pl.CostEstimate(
            flops=rows * columns, bytes_accessed=6 * rows * columns, transcendentals=0
        ),
        compiler_params=pltpu.CompilerParams(vmem_limit_bytes=50 << 20),
    )(bits[name].astype(jnp.int32).reshape(1), kept.reshape(shape), arrived.reshape(shape))
    return send.reshape(rows // 2, columns), keep.reshape(rows // 2, columns)


def cross(p, step, send):
    return lax.ppermute(send, ("emb", "seq"), AXIS_PAIRS[ORDERS[p][step]])


def copy_kernel(in_ref, out_ref):
    out_ref[...] = in_ref[...]


def copy_out(values):
    return pl.pallas_call(
        copy_kernel,
        grid=(4,),
        out_shape=jax.ShapeDtypeStruct(values.shape, values.dtype),
        in_specs=[pl.BlockSpec((32, 32, 128), lambda k: (k, 0, 0))],
        out_specs=pl.BlockSpec((32, 32, 128), lambda k: (k, 0, 0)),
    )(values)


def swap(send):
    return lax.ppermute(send, ("emb", "seq"), CORE_PAIRS)


def gradient_shares(core, turned, pre_grads, gated_turned, cotangent, bits, row_grads):
    keeps, arrived = [None] * 3, [None] * 3
    pre_y, pre_x, pre_z = pre_grads
    send_y, keep_y = run_weight_grads(core, turned, pre_y)
    send_y, pre_x = lax.optimization_barrier((send_y, pre_x))
    got_y = swap(send_y)
    send_x, keep_x = run_weight_grads(core, turned, pre_x)
    got_x = swap(send_x)
    send_x, got_y = lax.optimization_barrier((send_x, got_y))
    send, keeps[0] = halve(0, 0, keep_y, got_y, bits)
    send, pre_z = lax.optimization_barrier((send, pre_z))
    arrived[0] = cross(0, 0, send)
    send_z, keep_z = run_weight_grads(core, turned, pre_z, gated_turned, cotangent)
    got_z = swap(send_z)
    send_z, got_x = lax.optimization_barrier((send_z, got_x))
    send, keeps[1] = halve(1, 0, keep_x, got_x, bits)
    arrived[1] = cross(1, 0, send)
    send, got_z, row_grads = lax.optimization_barrier((send, got_z, row_grads))
    send, keeps[2] = halve(2, 0, keep_z, got_z, bits)
    arrived[2] = cross(2, 0, send)
    row_grads = copy_out(row_grads)
    for step in (1, 2):
        for p in range(3):
            send, keeps[p] = halve(p, step, keeps[p], arrived[p], bits)
            arrived[p] = cross(p, step, send)
        if step == 1:
            *arrived, row_grads = lax.optimization_barrier((*arrived, row_grads))
    total = jnp.concatenate(
        [
            (keeps[p].astype(F32) + arrived[p].astype(F32)).astype(BF16).reshape(8, 8, -1)
            for p in range(3)
        ],
        axis=2,
    )
    total = lax.all_to_all(total, ("emb", "seq"), 0, 0, tiled=True, axis_index_groups=cubes())
    return jnp.sum(total.astype(F32), axis=0), row_grads


def shards(
    item_ids, action_ids, hist_len, hist_owner, item_table, action_table, w_in, w_out, cotangent
):
    emb_count = lax.axis_size("emb")
    seq_count = lax.axis_size("seq")
    device_count = emb_count * seq_count
    owner_count = item_ids.shape[0]
    slot_rows = item_ids.shape[1]
    column_width = item_table.shape[1]
    looked = run_lookup(item_ids, action_ids, item_table, action_table)
    arrived = lax.all_to_all(looked, ("emb", "seq"), split_axis=0, concat_axis=0, tiled=True)
    arrived = arrived.reshape(emb_count, seq_count, slot_rows, column_width)
    owner_index = lax.axis_index(("emb", "seq"))
    slot_start, occupied = slot_layout(hist_len, hist_owner, owner_index, CAP)
    first = jnp.where(occupied, slot_start, CAP).astype(jnp.int32)[:, None]
    emb, seq = lax.axis_index("emb"), lax.axis_index("seq")
    bits = {
        "y1": emb // 4, "y0": emb // 2 % 2,
        "x1": seq // 8, "x0": seq // 4 % 2, "z1": seq // 2 % 2, "z0": seq % 2,
    }
    core = (emb % 2).astype(jnp.int32).reshape(1)
    gated_grad = mm_nt(cotangent, w_out).astype(BF16)
    outgoing, result, turned, gated_turned, *pre_grads = run_layer(
        core, arrived, first, cotangent, gated_grad, w_in, w_out
    )
    outgoing = outgoing.reshape(owner_count, slot_rows, column_width)
    row_grads = lax.all_to_all(outgoing, ("emb", "seq"), split_axis=0, concat_axis=0, tiled=True)
    sums, row_grads = gradient_shares(
        core, turned, pre_grads, gated_turned, cotangent, bits, row_grads
    )
    in_share, out_share = sums[:, : 4 * D], sums[:, 4 * D :]
    return (result, row_grads, in_share / device_count, out_share / device_count)


def solution(mesh):
    in_specs = (
        P(None, "seq"),
        P(None, "seq"),
        P(),
        P(),
        P(None, "emb"),
        P(None, "emb"),
        P(),
        P(),
        P(("emb", "seq"), None),
    )
    out_specs = (
        P(("emb", "seq"), None),
        P(None, "seq", "emb"),
        P(("emb", "seq"), None),
        P(("emb", "seq"), None),
    )
    return jax.shard_map(shards, mesh=mesh, in_specs=in_specs, out_specs=out_specs, check_vma=False)
```
